512 devices in a mesh: ctx: 64 (over z, x), head: 8 (over y, core).
Axes of the slice: x: 4, y: 4, z: 16, core: 2. Of those that a mesh axis runs over, the one named last changes fastest.
Arguments:
- queries: float32 [32768, 2048], P('ctx', 'head'), may hold values from -1024 to 1024
- keys: float32 [32768, 128], P('ctx'), may hold values from -1024 to 1024
- values: float32 [32768, 128], P('ctx'), may hold values from -6 to 6
- cotangent: float32 [32768, 2048], P('ctx', 'head'), may hold values from -384 to 384
- source_ids: int32 [32768], P('ctx'), may hold values from 0 to 63
- source_weights: float32 [64], replicated, may hold values from 0.25 to 4
- q_feature: float32 [16, 128, 128], P('head'), may hold values from -4 to 4
- k_feature: float32 [128, 128], replicated, may hold values from -4 to 4
Outputs:
- grad_queries: float32 [32768, 2048], P('ctx', 'head')
- grad_keys: float32 [32768, 128], P(('ctx', 'head'))
- grad_values: float32 [32768, 128], P(('ctx', 'head'))
- grad_q_feature: float32 [16, 128, 128], P('head')
- grad_k_feature: float32 [128, 128], replicated
The draws below stay inside these ranges and needn't reach their ends.
All inputs are finite; a program needn't handle non-finite values.
Results may differ from the reference program's by a relative error of at most 0.0015.
Values sent between devices are 32-bit elements; how exact they have to be, the bound alone decides.
A program may use at most 64 MiB of HBM per device.

```python
import math
import jax
import jax.numpy as jnp
import numpy as np
from jax import lax

D = 128
F = 128
HQ = 16
TOK_DEV = 512
TOKENS = 32768
SOURCES = 64


def feature_table(key, count):
    table = jax.random.normal(key, (count, D, F), jnp.float32)
    return jnp.clip(table, -6.0, 6.0) * (3.0 * D ** (-0.5))


def draw_q_feature(key, part):
    return feature_table(jax.random.fold_in(key, 101), HQ)


def draw_k_feature(key, part):
    return feature_table(jax.random.fold_in(key, 102), 1)[0]


def drawn_rows(key, count_rows, count_heads):
    subkeys = jax.random.split(key, 1)
    base = jnp.clip(jax.random.normal(subkeys[0], (count_rows, count_heads, D), jnp.float32), -6.0, 6.0)
    return base


def draw_queries(key, part):
    return drawn_rows(jax.random.fold_in(key, 201), TOKENS, HQ).reshape(TOKENS, HQ * D)


def draw_keys(key, part):
    return drawn_rows(jax.random.fold_in(key, 202), TOKENS, 1).reshape(TOKENS, D)


def plant(drawn, rng, least, largest):
    shape = drawn.shape
    index_at = [jax.random.randint(jax.random.fold_in(rng, axis), (), 0, shape[axis]) for axis in range(len(shape))]
    drawn = drawn.at[tuple(index_at)].set(least)
    longest = shape.index(max(shape))
    index_at[longest] = (index_at[longest] + 1) % shape[longest]
    return drawn.at[tuple(index_at)].set(largest)


def level_of(stream_key, shape, shards, low, high):
    def one(dim, blocks):
        draws = jax.random.uniform(jax.random.fold_in(jax.random.fold_in(stream_key, 6), dim), (blocks,), jnp.float32, low / len(shards), high / len(shards))
        return jnp.repeat(jnp.exp(draws), shape[dim] // blocks).reshape((-1,) + (1,) * (len(shape) - dim - 1))

    factor_of = one(*shards[0])
    for cut in shards[1:]:
        factor_of = factor_of * one(*cut)
    return factor_of


def rank_table(amount, skew):
    weights = [(1 << 20) // math.isqrt(grade ** skew) + 1 for grade in range(1, amount + 1)]
    deviation = 1 + sum(weights) // (1 << 30)
    return np.cumsum(np.array([max(1, weight // deviation) for weight in weights]))


def skewed_ids(own_key, shape, count, skew):
    listing = rank_table(count, skew)
    lot = jax.random.randint(jax.random.fold_in(own_key, 1), shape, 0, int(listing[count - 1]))
    standing = jnp.searchsorted(jnp.asarray(listing, jnp.int32), lot, side="right")
    return jax.random.permutation(jax.random.fold_in(own_key, 2), count)[standing].astype(jnp.int32)


def normal_values(stream_key, shape, width, limit, pieces=(), kind=jnp.bfloat16):
    result = width * jax.random.normal(stream_key, shape, jnp.float32)
    if pieces:
        result = result * level_of(stream_key, shape, pieces, -0.22, 0.18)
    return jnp.clip(result, -limit, limit).astype(kind)


def setup_inputs(seed: int = 0) -> dict:
    seeds = jax.random.split(jax.random.key(seed), 9)
    queries = draw_queries(jax.random.fold_in(seeds[8], 71), 0)
    keys = draw_keys(jax.random.fold_in(seeds[8], 71), 0)
    values = normal_values(seeds[2], (TOKENS, D), 1.0, 6.0, ((0, 64),), jnp.float32)
    cotangent = normal_values(seeds[3], (TOKENS, HQ * D), 64.0, 384.0, ((0, 64), (1, 8)), jnp.float32)
    source_ids = plant(skewed_ids(seeds[4], (TOKENS,), SOURCES, 2), jax.random.fold_in(seeds[4], 3), 0, SOURCES - 1).astype(jnp.int32)
    source_weights = jnp.clip(jnp.exp(jax.random.uniform(seeds[5], (SOURCES,), jnp.float32, math.log(0.25), math.log(4.0))), 0.25, 4.0)
    q_feature = draw_q_feature(jax.random.fold_in(seeds[8], 71), 0)
    k_feature = draw_k_feature(jax.random.fold_in(seeds[8], 71), 0)
    return {"queries": queries, "keys": keys, "values": values, "cotangent": cotangent, "source_ids": source_ids, "source_weights": source_weights, "q_feature": q_feature, "k_feature": k_feature}


def matmul(left, right):
    return jnp.dot(left, right, precision=lax.Precision.HIGHEST, preferred_element_type=jnp.float32)


def feature_map(inputs, weight):
    logits = matmul(inputs, weight)
    upper = jax.nn.softmax(logits, axis=-1)
    lower = jax.nn.softmax(-logits, axis=-1)
    return jnp.concatenate([upper, lower], axis=-1), upper, lower


def feature_back(inputs, weight, upper, lower, grad_feat):
    half = upper.shape[-1]
    grad_upper = grad_feat[:, :half]
    grad_lower = grad_feat[:, half:]
    grad_logits = upper * (grad_upper - jnp.sum(upper * grad_upper, axis=-1, keepdims=True))
    grad_logits = grad_logits - lower * (grad_lower - jnp.sum(lower * grad_lower, axis=-1, keepdims=True))
    return matmul(grad_logits, weight.T), matmul(inputs.T, grad_logits)


def causal_mask(count):
    row_index = lax.broadcasted_iota(jnp.int32, (count, count), 0)
    col_index = lax.broadcasted_iota(jnp.int32, (count, count), 1)
    return (row_index >= col_index).astype(jnp.float32)


def block_terms(query_feat, key_feat, value_rows, scaled, earlier, earlier_totals):
    lower_mask = causal_mask(query_feat.shape[0])
    scores = matmul(query_feat, key_feat.T) * lower_mask
    numerator = matmul(scores, value_rows) + matmul(query_feat, earlier)
    normalizer = jnp.sum(scores, axis=1) + matmul(query_feat, earlier_totals)
    output = numerator / normalizer[:, None]
    grad_numer = scaled / normalizer[:, None]
    grad_norm = -jnp.sum(scaled * output, axis=1) / normalizer
    grad_scores = (matmul(grad_numer, value_rows.T) + grad_norm[:, None]) * lower_mask
    grad_query = matmul(grad_scores, key_feat) + matmul(grad_numer, earlier.T) + grad_norm[:, None] * earlier_totals[None, :]
    grad_key = matmul(grad_scores.T, query_feat)
    grad_value = matmul(scores.T, grad_numer)
    carried = matmul(query_feat.T, grad_numer)
    carried_totals = matmul(grad_norm[None, :], query_feat)[0]
    return grad_query, grad_key, grad_value, carried, carried_totals


def reference(queries, keys, values, cotangent, source_ids, source_weights, q_feature, k_feature):
    count = queries.shape[0]
    blocks = count // TOK_DEV
    features = 2 * F
    weight = source_weights[source_ids]
    key_feat, key_upper, key_lower = feature_map(keys, k_feature)
    key_blocks = key_feat.reshape(blocks, TOK_DEV, features)
    value_blocks = values.reshape(blocks, TOK_DEV, D)
    grad_keyfeat = jnp.zeros((count, features), jnp.float32)
    grad_vals = jnp.zeros((count, D), jnp.float32)
    carried_all = jnp.zeros((blocks, features, D), jnp.float32)
    carried_tot = jnp.zeros((blocks, features), jnp.float32)
    query_grads = []
    weight_grads = []
    for head in range(HQ):
        query_head = queries[:, head * D:(head + 1) * D]
        query_feat, query_upper, query_lower = feature_map(query_head, q_feature[head])
        scaled = cotangent[:, head * D:(head + 1) * D] * weight[:, None]

        def advance(carry, inputs):
            earlier, earlier_totals = carry
            query_block, key_block, value_block, scaled_block = inputs
            terms = block_terms(query_block, key_block, value_block, scaled_block, earlier, earlier_totals)
            earlier = earlier + matmul(key_block.T, value_block)
            earlier_totals = earlier_totals + jnp.sum(key_block, axis=0)
            return (earlier, earlier_totals), terms

        start_state = (jnp.zeros((features, D), jnp.float32), jnp.zeros((features,), jnp.float32))
        inputs = (query_feat.reshape(blocks, TOK_DEV, features), key_blocks, value_blocks, scaled.reshape(blocks, TOK_DEV, D))
        _, outputs = lax.scan(advance, start_state, inputs)
        grad_query, grad_key, grad_value, carried, carried_totals = outputs
        grad_head, grad_weight = feature_back(query_head, q_feature[head], query_upper, query_lower, grad_query.reshape(count, features))
        query_grads.append(grad_head)
        weight_grads.append(grad_weight)
        grad_keyfeat = grad_keyfeat + grad_key.reshape(count, features)
        grad_vals = grad_vals + grad_value.reshape(count, D)
        carried_all = carried_all + carried
        carried_tot = carried_tot + carried_totals
    later = jnp.flip(jnp.cumsum(jnp.flip(carried_all, 0), axis=0), 0) - carried_all
    later_tot = jnp.flip(jnp.cumsum(jnp.flip(carried_tot, 0), axis=0), 0) - carried_tot
    inter_key = jnp.einsum("bte,bfe->btf", value_blocks, later, precision=lax.Precision.HIGHEST) + later_tot[:, None, :]
    inter_value = jnp.einsum("btf,bfe->bte", key_blocks, later, precision=lax.Precision.HIGHEST)
    grad_keyfeat = grad_keyfeat + inter_key.reshape(count, features)
    grad_vals = grad_vals + inter_value.reshape(count, D)
    grad_keys, grad_kweight = feature_back(keys, k_feature, key_upper, key_lower, grad_keyfeat)
    grad_queries = jnp.concatenate(query_grads, axis=1)
    grad_qweight = jnp.stack(weight_grads, axis=0)
    return grad_queries, grad_keys, grad_vals, grad_qweight, grad_kweight
```

```python
import jax
import jax.numpy as jnp
from jax import lax
from jax.experimental import pallas as pl
from jax.experimental.pallas import tpu as pltpu
from jax.sharding import PartitionSpec as P

MESH = pl.DeviceIdType.MESH
F32 = jnp.float32
BF16 = jnp.bfloat16
NN = ((1,), (0,))
NT = ((1,), (1,))
TN = ((0,), (0,))
XN = 4
ZN = 16
HN = 8
GN = XN * HN
ROWS = 512
CH = 256
D = 128
NC = ROWS // CH
OWN = ROWS // HN
TR = 2 * D // GN
TM = TR + 2
TP = TR + 8
KW = D // GN
QX = 2 * D // XN
QZ = QX // ZN


def split(a):
    high = a.astype(BF16)
    return high, (a - high.astype(F32)).astype(BF16)


def dot(a, b, dims):
    return lax.dot_general(a, b, (dims, ((), ())), preferred_element_type=F32)


def mm3(a, b, dims):
    (ah, al), (bh, bl) = a, b
    return dot(ah, bh, dims) + (dot(ah, bl, dims) + dot(al, bh, dims))


def total(parts):
    acc = parts[0]
    for i in range(1, XN):
        acc = acc + parts[i]
    return acc


def features(inputs, weight):
    logits = jnp.dot(inputs, weight, precision=lax.Precision.HIGHEST, preferred_element_type=F32)
    upper = jnp.exp(logits - jnp.max(logits, axis=1, keepdims=True))
    lower = jnp.exp(jnp.min(logits, axis=1, keepdims=True) - logits)
    upper = upper * (1.0 / jnp.sum(upper, axis=1, keepdims=True))
    lower = lower * (1.0 / jnp.sum(lower, axis=1, keepdims=True))
    return upper, lower


def back(upper, lower, a, b):
    up = upper * (a - jnp.sum(upper * a, axis=1, keepdims=True))
    return up - lower * (b - jnp.sum(lower * b, axis=1, keepdims=True))


def column(row):
    return jnp.transpose(jnp.broadcast_to(row, (D, D)))


def kernel(
    q_ref, k_ref, v_ref, c_ref, ids_ref, sw_ref, qw_ref, kw_ref,
    gq_ref, gk_ref, gv_ref, gqw_ref, gkw_ref,
    kf, kh, kl, vh, vl, qf, qh, ql, sh, sl, intra, scaled, st, gnh, gnl, gnorm, c1, gkf, gval,
    sa, ra, ta, za, gas, ga, cb, rb, tb, zb, gbs, gb, ks, kr, qs, rq, tq, zq, gzs, gz, gx, ck, rc, tc, zc, gcs, gc,
    s_one, s_two, r_one, r_two,
):
    pos = lax.axis_index("ctx")
    h = lax.axis_index("head")
    z = pos // XN
    x = pos % XN
    me = h * XN + x

    def group_peer(i):
        t = (me + i) % GN
        return t, t % XN, t // XN

    def each_group(act):
        def step(i, carry):
            act(*group_peer(i))
            return carry
        lax.fori_loop(1, GN, step, 0)

    barrier = pltpu.get_barrier_semaphore()

    def greet(ctx, head):
        pl.semaphore_signal(barrier, inc=1, device_id=(ctx, head), device_id_type=MESH)

    za[...] = jnp.zeros_like(za)
    zb[...] = jnp.zeros_like(zb)
    each_group(lambda t, xp, hp: greet(z * XN + xp, hp))

    def greet_z(i, carry):
        greet(((z + i) % ZN) * XN + x, h)
        return carry
    lax.fori_loop(1, ZN, greet_z, 0)

    def start(src, dst, ssem, rsem, ctx, head):
        pltpu.make_async_remote_copy(
            src_ref=src, dst_ref=dst, send_sem=ssem, recv_sem=rsem,
            device_id=(ctx, head), device_id_type=MESH,
        ).start()

    def drain(ref, sem):
        pltpu.make_async_copy(ref, ref, sem).wait()

    def send_group(src_of, dst, index):
        each_group(lambda t, xp, hp: start(
            src_of(t, xp, hp), dst.at[me], s_one.at[index], r_one.at[index], z * XN + xp, hp))

    def recv_group(dst, index):
        drain(dst.at[pl.ds(0, GN - 1)], r_one.at[index])

    def sent_group(dst, index):
        drain(dst.at[pl.ds(0, GN - 1)], s_one.at[index])

    def send_x(src_of, dst, index):
        def step(i, carry):
            xp = (x + i) % XN
            start(src_of(xp), dst.at[x], s_one.at[index], r_one.at[index], z * XN + xp, h)
            return carry
        lax.fori_loop(1, XN, step, 0)

    def recv_x(dst, index):
        drain(dst.at[pl.ds(0, XN - 1)], r_one.at[index])

    def sent_x(dst, index):
        drain(dst.at[pl.ds(0, XN - 1)], s_one.at[index])

    def send_z(src_of, dst, index, low, high):
        def step(zp, carry):
            @pl.when(zp != z)
            def _():
                start(src_of(zp), dst.at[z], s_two.at[index, zp], r_two.at[index, z], zp * XN + x, h)
            return carry
        lax.fori_loop(low, high, step, 0)

    def wait_z(dst, sems, index, low, high):
        def step(zp, carry):
            @pl.when(zp != z)
            def _():
                drain(dst.at[zp], sems.at[index, zp])
            return carry
        lax.fori_loop(low, high, step, 0)

    upper, lower = features(k_ref[...], kw_ref[...])
    kf[:, :D] = upper
    kf[:, D:] = lower
    kh[...], kl[...] = split(kf[...])
    vh[:, :D], vl[:, :D] = split(v_ref[...])
    vh[:, D:] = jnp.ones((ROWS, D), BF16)
    vl[:, D:] = jnp.zeros((ROWS, D), BF16)
    tot = []
    for c in range(NC):
        r = pl.ds(c * CH, CH)
        st[c] = mm3((kh[r, :], kl[r, :]), (vh[r, :D], vl[r, :D]), TN)
        tot.append((jnp.sum(kf[r, :D], axis=0, keepdims=True), jnp.sum(kf[r, D:], axis=0, keepdims=True)))
    tot_all = jnp.concatenate([tot[0][0] + tot[1][0], tot[0][1] + tot[1][1]], axis=0)
    mine = st[0, pl.ds(h * (XN * TR), XN * TR), :] + st[1, pl.ds(h * (XN * TR), XN * TR), :]
    for i in range(XN):
        sa[i, :TR] = mine[TR * i:TR * i + TR]
        sa[i, TR:TM] = tot_all
    pl.semaphore_wait(barrier, GN - 1 + ZN - 1)
    send_x(lambda xp: sa.at[xp, pl.ds(0, TM)], ra.at[:, pl.ds(0, TM)], 0)
    ra[x] = sa[x]

    ids = ids_ref[...]
    onehot = (lax.broadcasted_iota(jnp.int32, (64, ROWS), 0) == ids).astype(F32).astype(BF16)
    diag = lax.broadcasted_iota(jnp.int32, (64, 64), 0) == lax.broadcasted_iota(jnp.int32, (64, 64), 1)
    wcol = jnp.sum(jnp.where(diag, sw_ref[...], 0.0), axis=1, keepdims=True)
    wtab = jnp.broadcast_to(wcol, (64, D))
    w1, rest = wtab.astype(BF16), wtab - wtab.astype(BF16).astype(F32)
    w2, w3 = split(rest)
    weight = dot(onehot, w1, TN) + dot(onehot, w2, TN) + dot(onehot, w3, TN)
    mask = lax.broadcasted_iota(jnp.int32, (CH, CH), 0) >= lax.broadcasted_iota(jnp.int32, (CH, CH), 1)

    def before(n):
        lanes = pl.ds(n * D, D)
        scaled[n] = c_ref[:, lanes] * weight
        upper, lower = features(q_ref[:, lanes], qw_ref[n])
        qf[n, :, :D] = upper
        qf[n, :, D:] = lower
        qh[n], ql[n] = split(qf[n])
        for c in range(NC):
            r = pl.ds(c * CH, CH)
            s = mm3((qh[n, r, :], ql[n, r, :]), (kh[r, :], kl[r, :]), NT)
            sh[n, r, :], sl[n, r, :] = split(jnp.where(mask, s, 0.0))
            intra[n, r, :] = mm3((sh[n, r, :], sl[n, r, :]), (vh[r, :], vl[r, :]), NN)

    recv_x(ra.at[:, pl.ds(0, TM)], 0)
    ta[...] = total(ra)
    send_z(lambda zp: ta.at[pl.ds(0, TM)], za.at[:, pl.ds(0, TM)], 0, z + 1, ZN)
    before(0)
    wait_z(za.at[:, pl.ds(0, TM)], r_two, 0, 0, z)
    pre = jnp.sum(za[...], axis=0)
    pre_tot = pre[TR:TM]
    for i in range(XN):
        gas[i] = pre[:TR]
        if i < XN - 1:
            pre = pre + ra[i]
            pre_tot = pre_tot + jnp.where(i < x, ra[i, TR:TM], 0.0)
    send_group(lambda t, xp, hp: gas.at[xp], ga, 1)
    ga[me] = gas[x]
    before(1)
    recv_group(ga, 1)

    p_now = ga[...].reshape(2 * D, D)
    tot_now = (pre_tot[0:1], pre_tot[1:2])
    states, totals = [], []
    for c in range(NC):
        states.append(split(p_now))
        totals.append(tot_now)
        if c < NC - 1:
            p_now = p_now + st[c]
            tot_now = (tot_now[0] + tot[c][0], tot_now[1] + tot[c][1])
    ct = [[0.0, 0.0] for _ in range(NC)]
    carried = []
    for c in range(NC):
        r = pl.ds(c * CH, CH)
        thi, tlo = split(jnp.concatenate([column(totals[c][0]), column(totals[c][1])], axis=0))
        full = (jnp.concatenate([states[c][0], thi], axis=1), jnp.concatenate([states[c][1], tlo], axis=1))
        acc = None
        for n in range(2):
            q = (qh[n, r, :], ql[n, r, :])
            nn = intra[n, r, :] + mm3(q, full, NN)
            inv = 1.0 / nn[:, D:]
            sc = scaled[n, r, :]
            gnum = sc * inv
            gno = -jnp.sum(sc * (nn[:, :D] * inv), axis=1, keepdims=True) * inv
            gnorm[n, r, :] = gno
            g = split(gnum)
            gnh[n, r, :], gnl[n, r, :] = g
            ct[c][0] = ct[c][0] + jnp.sum(gno * qf[n, r, :D], axis=0, keepdims=True)
            ct[c][1] = ct[c][1] + jnp.sum(gno * qf[n, r, D:], axis=0, keepdims=True)
            term = mm3(q, g, TN)
            acc = term if acc is None else acc + term
        carried.append(acc)
    c1[...] = carried[1]
    whole = carried[0] + carried[1]
    ct_all = jnp.concatenate([ct[0][0] + ct[1][0], ct[0][1] + ct[1][1]], axis=0)
    for t in range(GN):
        cb[t, :TR] = whole[TR * t:TR * t + TR]
        cb[t, TR:TM] = ct_all
    send_group(lambda t, xp, hp: cb.at[t, pl.ds(0, TM)], rb.at[:, pl.ds(0, TM)], 2)
    rb[me] = cb[me]

    def after(n):
        lanes = pl.ds(n * D, D)
        wpair = split(qw_ref[n])
        xs = split(q_ref[:, lanes])
        grads = []
        for c in range(NC):
            r = pl.ds(c * CH, CH)
            g = (gnh[n, r, :], gnl[n, r, :])
            gno = gnorm[n, r, :]
            gs = mm3(g, (vh[r, :D], vl[r, :D]), NT) + jnp.concatenate([gno, gno], axis=1)
            gs = split(jnp.where(mask, gs, 0.0))
            gfeat = mm3(gs, (kh[r, :], kl[r, :]), NN) + mm3(g, states[c], NT)
            a = gfeat[:, :D] + gno * totals[c][0]
            b = gfeat[:, D:] + gno * totals[c][1]
            gl = split(back(qf[n, r, :D], qf[n, r, D:], a, b))
            grads.append(gl)
            gq_ref[r, lanes] = mm3(gl, wpair, NT)
            gk = mm3(gs, (qh[n, r, :], ql[n, r, :]), TN)
            gv = mm3((sh[n, r, :], sl[n, r, :]), g, TN)
            if n == 0:
                gkf[r, :] = gk
                gval[r, :] = gv
            else:
                gkf[r, :] += gk
                gval[r, :] += gv
        gl = (jnp.concatenate([g[0] for g in grads], axis=0), jnp.concatenate([g[1] for g in grads], axis=0))
        gw = mm3(xs, gl, TN)
        parts = XN // 2
        for i in range(parts):
            qs[parts * n + i] = gw[QX * i:QX * i + QX]

    after(0)
    recv_group(rb.at[:, pl.ds(0, TM)], 2)
    by_x = []
    for i in range(XN):
        s = rb[i]
        for hp in range(1, HN):
            s = s + rb[hp * XN + i]
        by_x.append(s)
    tb[...] = total(by_x)
    send_z(lambda zp: tb.at[pl.ds(0, TM)], zb.at[:, pl.ds(0, TM)], 1, 0, z)
    after(1)
    send_x(lambda xp: qs.at[xp], rq, 3)
    rq[x] = qs[x]

    wait_z(zb.at[:, pl.ds(0, TM)], r_two, 1, z + 1, ZN)
    suf = jnp.sum(zb[...], axis=0)
    suf_tot = suf[TR:TM]
    for i in reversed(range(XN)):
        gbs[i] = suf[:TR]
        if i > 0:
            suf = suf + by_x[i]
            suf_tot = suf_tot + jnp.where(i > x, by_x[i][TR:TM], 0.0)
    send_group(lambda t, xp, hp: gbs.at[xp], gb, 4)
    gb[me] = gbs[x]

    r = pl.ds(0, CH)
    cpair = split(c1[...])
    gkf[r, :] += mm3((vh[r, :D], vl[r, :D]), cpair, NT) + jnp.concatenate([ct[1][0], ct[1][1]], axis=1)
    gval[r, :] += mm3((kh[r, :], kl[r, :]), cpair, NN)
    gl = back(kf[:, :D], kf[:, D:], gkf[:, :D], gkf[:, D:])
    for i in range(HN):
        ks[i, :, :D] = gl[OWN * i:OWN * i + OWN]
        ks[i, :, D:] = gval[OWN * i:OWN * i + OWN, :]

    def send_key(i, carry):
        hp = (h + i) % HN
        start(ks.at[hp], kr.at[h], s_one.at[5], r_one.at[5], pos, hp)
        return carry
    lax.fori_loop(1, HN, send_key, 0)
    kr[h] = ks[h]

    recv_x(rq, 3)
    tsum = total(rq)
    for i in range(ZN):
        tq[i] = tsum[QZ * i:QZ * i + QZ]
    send_z(lambda zp: tq.at[zp], zq, 2, 0, ZN)
    zq[z] = tq[z]

    recv_group(gb, 4)
    later = split(gb[...].reshape(2 * D, D))
    own = pl.ds(h * OWN, OWN)
    v64 = (vh[own, :D], vl[own, :D])
    gfeat = mm3(v64, later, NT)
    gval64 = mm3((kh[own, :], kl[own, :]), later, NN)
    gl = back(kf[own, :D], kf[own, D:], gfeat[:, :D] + suf_tot[0:1], gfeat[:, D:] + suf_tot[1:2])
    drain(kr.at[pl.ds(0, HN - 1)], r_one.at[5])
    got = kr[0]
    for i in range(1, HN):
        got = got + kr[i]
    glp = split(gl + got[:, :D])
    gkw = mm3(split(k_ref[own, :]), glp, TN)
    for i in range(GN):
        ck[i] = gkw[KW * i:KW * i + KW]
    send_group(lambda t, xp, hp: ck.at[t], rc, 6)
    rc[me] = ck[me]
    gk_ref[...] = mm3(glp, split(kw_ref[...]), NT)
    gv_ref[...] = gval64 + got[:, D:]

    wait_z(zq, r_two, 2, 0, ZN)
    gzs[...] = jnp.sum(zq[...], axis=0)
    send_z(lambda zp: gzs, gz, 3, 0, ZN)
    gz[z] = gzs[...]

    recv_group(rc, 6)
    tc[...] = jnp.sum(rc[...], axis=0)
    send_z(lambda zp: tc, zc, 4, 0, ZN)
    zc[z] = tc[...]

    wait_z(gz, r_two, 3, 0, ZN)
    send_x(lambda xp: gz, gx, 7)
    gx[x] = gz[...]

    wait_z(zc, r_two, 4, 0, ZN)
    gcs[...] = jnp.sum(zc[...], axis=0)
    send_group(lambda t, xp, hp: gcs, gc, 8)
    gc[me] = gcs[...]

    recv_x(gx, 7)
    for i in range(XN):
        for j in range(ZN):
            row = QX * i + QZ * j
            gqw_ref[row // D, row % D:row % D + QZ, :] = gx[i, j]
    recv_group(gc, 8)
    for i in range(GN):
        gkw_ref[KW * i:KW * i + KW, :] = gc[i]

    sent_x(ra.at[:, pl.ds(0, TM)], 0)
    sent_group(ga, 1)
    sent_group(rb.at[:, pl.ds(0, TM)], 2)
    sent_x(rq, 3)
    sent_group(gb, 4)
    drain(kr.at[pl.ds(0, HN - 1)], s_one.at[5])
    sent_group(rc, 6)
    sent_x(gx, 7)
    sent_group(gc, 8)
    wait_z(za.at[:, pl.ds(0, TM)], s_two, 0, z + 1, ZN)
    wait_z(zb.at[:, pl.ds(0, TM)], s_two, 1, 0, z)
    wait_z(zq, s_two, 2, 0, ZN)
    wait_z(gz, s_two, 3, 0, ZN)
    wait_z(zc, s_two, 4, 0, ZN)


def on_device(queries, keys, values, cotangent, source_ids, source_weights, q_feature, k_feature):
    def vm(*shape, dtype=F32):
        return pltpu.VMEM(shape, dtype)

    b = dict(dtype=BF16)
    vmem = pl.BlockSpec(memory_space=pltpu.VMEM)
    return pl.pallas_call(
        kernel,
        out_shape=(
            jax.ShapeDtypeStruct((ROWS, 2 * D), F32),
            jax.ShapeDtypeStruct((OWN, D), F32),
            jax.ShapeDtypeStruct((OWN, D), F32),
            jax.ShapeDtypeStruct((2, D, D), F32),
            jax.ShapeDtypeStruct((D, D), F32),
        ),
        in_specs=[vmem] * 8,
        out_specs=[vmem] * 5,
        scratch_shapes=[
            vm(ROWS, 2 * D), vm(ROWS, 2 * D, **b), vm(ROWS, 2 * D, **b),
            vm(ROWS, 2 * D, **b), vm(ROWS, 2 * D, **b),
            vm(2, ROWS, 2 * D), vm(2, ROWS, 2 * D, **b), vm(2, ROWS, 2 * D, **b),
            vm(2, ROWS, CH, **b), vm(2, ROWS, CH, **b),
            vm(2, ROWS, 2 * D), vm(2, ROWS, D), vm(NC, 2 * D, D),
            vm(2, ROWS, D, **b), vm(2, ROWS, D, **b), vm(2, ROWS, D),
            vm(2 * D, D), vm(ROWS, 2 * D), vm(ROWS, D),
            vm(XN, TP, D), vm(XN, TP, D), vm(TP, D), vm(ZN, TP, D), vm(XN, TR, D), vm(GN, TR, D),
            vm(GN, TP, D), vm(GN, TP, D), vm(TP, D), vm(ZN, TP, D), vm(XN, TR, D), vm(GN, TR, D),
            vm(HN, OWN, 2 * D), vm(HN, OWN, 2 * D),
            vm(XN, QX, D), vm(XN, QX, D), vm(ZN, QZ, D), vm(ZN, QZ, D),
            vm(QZ, D), vm(ZN, QZ, D), vm(XN, ZN, QZ, D),
            vm(GN, KW, D), vm(GN, KW, D), vm(KW, D), vm(ZN, KW, D), vm(KW, D), vm(GN, KW, D),
            pltpu.SemaphoreType.DMA((9,)),
            pltpu.SemaphoreType.DMA((5, ZN)),
            pltpu.SemaphoreType.DMA((9,)),
            pltpu.SemaphoreType.DMA((5, ZN)),
        ],
        compiler_params=pltpu.CompilerParams(
            collective_id=0, has_side_effects=True, vmem_limit_bytes=48 * 1024 * 1024
        ),
        cost_estimate=pl.CostEstimate(flops=3_000_000_000, bytes_accessed=2_500_000, transcendentals=400_000),
    )(queries, keys, values, cotangent, source_ids.reshape(1, ROWS), source_weights.reshape(1, -1), q_feature, k_feature)


def solution(mesh):
    placed = (
        P("ctx", "head"),
        P("ctx", None),
        P("ctx", None),
        P("ctx", "head"),
        P("ctx"),
        P(),
        P("head", None, None),
        P(),
    )
    return jax.shard_map(
        on_device,
        mesh=mesh,
        in_specs=placed,
        out_specs=(
            P("ctx", "head"),
            P(("ctx", "head"), None),
            P(("ctx", "head"), None),
            P("head", None, None),
            P(),
        ),
        check_vma=False,
    )
```

```python
import jax
import jax.numpy as jnp
from jax import lax
from jax.experimental import pallas as pl
from jax.experimental.pallas import tpu as pltpu
from jax.sharding import PartitionSpec as P

MESH = pl.DeviceIdType.MESH
F32 = jnp.float32
BF16 = jnp.bfloat16
NN = ((1,), (0,))
NT = ((1,), (1,))
TN = ((0,), (0,))
XN = 4
ZN = 16
HN = 8
GN = XN * HN
ROWS = 512
CH = 256
D = 128
NC = ROWS // CH
OWN = ROWS // HN
TR = 2 * D // GN
TM = TR + 2
TP = TR + 8
KW = D // GN
QX = 2 * D // XN
QZ = QX // ZN


def split(a):
    high = a.astype(BF16)
    return high, (a - high.astype(F32)).astype(BF16)


def dot(a, b, dims):
    return lax.dot_general(a, b, (dims, ((), ())), preferred_element_type=F32)


def mm3(a, b, dims):
    (ah, al), (bh, bl) = a, b
    return dot(ah, bh, dims) + (dot(ah, bl, dims) + dot(al, bh, dims))


def total(parts):
    acc = parts[0]
    for i in range(1, XN):
        acc = acc + parts[i]
    return acc


def features(inputs, weight):
    logits = jnp.dot(inputs, weight, precision=lax.Precision.HIGHEST, preferred_element_type=F32)
    upper = jnp.exp(logits - jnp.max(logits, axis=1, keepdims=True))
    lower = jnp.exp(jnp.min(logits, axis=1, keepdims=True) - logits)
    upper = upper * (1.0 / jnp.sum(upper, axis=1, keepdims=True))
    lower = lower * (1.0 / jnp.sum(lower, axis=1, keepdims=True))
    return upper, lower


def back(upper, lower, a, b):
    up = upper * (a - jnp.sum(upper * a, axis=1, keepdims=True))
    return up - lower * (b - jnp.sum(lower * b, axis=1, keepdims=True))


def column(row):
    return jnp.transpose(jnp.broadcast_to(row, (D, D)))


def swing(i, n):
    return (n // 2 + ((i + 1) // 2) * (1 - 2 * (i % 2))) % n


def kernel(
    q_in, k_in, v_in, c_in, ids_in, sw_in, qw_in, kw_in,
    gq_out, gk_out, gv_out, gqw_out, gkw_out,
    gq_ref, gk_ref, gv_ref, gqw_ref, gkw_ref, o_sem,
    q_ref, k_ref, v_ref, c_ref, ids_ref, sw_ref, qw_ref, kw_ref, i_sem,
    kf, kh, kl, vh, vl, qf, qh, ql, sh, sl, intra, scaled, st, gnh, gnl, gnorm, c1, gkf, gval,
    sa, ra, ta, za, gas, ga, cb, rb, tb, zb, gbs, gb, ks, kr, qs, rq, tq, zq, gzs, gz, gx, ck, rc, tc, zc, gcs, gc,
    qth, qtl, kth, ktl, iks, ikr, gint,
    s_one, s_two, r_one, r_two,
):
    pos = lax.axis_index("ctx")
    h = lax.axis_index("head")
    z = pos // XN
    x = pos % XN
    me = h * XN + x

    def each_group(act):
        def step(i, carry):
            xp = (x + swing(i // HN, XN)) % XN
            yp = (h // 2 + swing(i // 2 % (HN // 2), HN // 2)) % (HN // 2)
            hp = yp * 2 + (h + i + 1) % 2
            act(hp * XN + xp, xp, hp)
            return carry
        lax.fori_loop(0, GN - 1, step, 0)

    def each_z(act):
        def step(i, carry):
            act((z + swing(i, ZN)) % ZN)
            return carry
        lax.fori_loop(0, ZN - 1, step, 0)

    barrier = pltpu.get_barrier_semaphore()

    def greet(ctx, head):
        pl.semaphore_signal(barrier, inc=1, device_id=(ctx, head), device_id_type=MESH)

    loads = [
        pltpu.make_async_copy(src, dst, i_sem.at[i])
        for i, (src, dst) in enumerate([
            (k_in, k_ref), (kw_in, kw_ref), (v_in, v_ref), (q_in, q_ref),
            (qw_in, qw_ref), (c_in, c_ref), (ids_in, ids_ref), (sw_in, sw_ref),
        ])
    ]
    for load in loads:
        load.start()
    stores = [
        pltpu.make_async_copy(src, dst, o_sem.at[i])
        for i, (src, dst) in enumerate([
            (gq_ref, gq_out), (gk_ref, gk_out), (gv_ref, gv_out), (gqw_ref, gqw_out), (gkw_ref, gkw_out),
        ])
    ]
    za[...] = jnp.zeros_like(za)
    zb[...] = jnp.zeros_like(zb)
    each_z(lambda zp: greet(zp * XN + x, h))
    each_group(lambda t, xp, hp: greet(z * XN + xp, hp))

    def start(src, dst, ssem, rsem, ctx, head):
        pltpu.make_async_remote_copy(
            src_ref=src, dst_ref=dst, send_sem=ssem, recv_sem=rsem,
            device_id=(ctx, head), device_id_type=MESH,
        ).start()

    def drain(ref, sem):
        pltpu.make_async_copy(ref, ref, sem).wait()

    def send_group(src_of, dst, index):
        each_group(lambda t, xp, hp: start(
            src_of(t, xp, hp), dst.at[me], s_one.at[index], r_one.at[index], z * XN + xp, hp))

    def recv_group(dst, index):
        drain(dst.at[pl.ds(0, GN - 1)], r_one.at[index])

    def sent_group(dst, index):
        drain(dst.at[pl.ds(0, GN - 1)], s_one.at[index])

    def send_x(src_of, dst, index):
        def step(i, carry):
            xp = (x + swing(i, XN)) % XN
            start(src_of(xp), dst.at[x], s_one.at[index], r_one.at[index], z * XN + xp, h)
            return carry
        lax.fori_loop(0, XN - 1, step, 0)

    def recv_x(dst, index):
        drain(dst.at[pl.ds(0, XN - 1)], r_one.at[index])

    def sent_x(dst, index):
        drain(dst.at[pl.ds(0, XN - 1)], s_one.at[index])

    def send_z(src_of, dst, index, low, high):
        def act(zp):
            @pl.when((zp >= low) & (zp < high))
            def _():
                start(src_of(zp), dst.at[z], s_two.at[index, zp], r_two.at[index, z], zp * XN + x, h)
        each_z(act)

    def wait_z(dst, sems, index, low, high):
        def step(zp, carry):
            @pl.when(zp != z)
            def _():
                drain(dst.at[zp], sems.at[index, zp])
            return carry
        lax.fori_loop(low, high, step, 0)

    loads[0].wait()
    loads[1].wait()
    upper, lower = features(k_ref[...], kw_ref[...])
    kf[:, :D] = upper
    kf[:, D:] = lower
    kh[...], kl[...] = split(kf[...])
    loads[2].wait()
    vh[:, :D], vl[:, :D] = split(v_ref[...])
    vh[:, D:] = jnp.ones((ROWS, D), BF16)
    vl[:, D:] = jnp.zeros((ROWS, D), BF16)
    tot = []
    for c in range(NC):
        r = pl.ds(c * CH, CH)
        st[c] = mm3((kh[r, :], kl[r, :]), (vh[r, :D], vl[r, :D]), TN)
        tot.append((jnp.sum(kf[r, :D], axis=0, keepdims=True), jnp.sum(kf[r, D:], axis=0, keepdims=True)))
    tot_all = jnp.concatenate([tot[0][0] + tot[1][0], tot[0][1] + tot[1][1]], axis=0)
    mine = st[0, pl.ds(h * (XN * TR), XN * TR), :] + st[1, pl.ds(h * (XN * TR), XN * TR), :]
    for i in range(XN):
        sa[i, :TR] = mine[TR * i:TR * i + TR]
        sa[i, TR:TM] = tot_all
    pl.semaphore_wait(barrier, GN - 1 + ZN - 1)
    send_x(lambda xp: sa.at[xp, pl.ds(0, TM)], ra.at[:, pl.ds(0, TM)], 0)
    ra[x] = sa[x]

    for load in loads[3:]:
        load.wait()
    kth[...], ktl[...] = split(jnp.transpose(k_ref[...]))

    ids = ids_ref[...]
    onehot = (lax.broadcasted_iota(jnp.int32, (64, ROWS), 0) == ids).astype(F32).astype(BF16)
    diag = lax.broadcasted_iota(jnp.int32, (64, 64), 0) == lax.broadcasted_iota(jnp.int32, (64, 64), 1)
    wcol = jnp.sum(jnp.where(diag, sw_ref[...], 0.0), axis=1, keepdims=True)
    wtab = jnp.broadcast_to(wcol, (64, D))
    w1, rest = wtab.astype(BF16), wtab - wtab.astype(BF16).astype(F32)
    w2, w3 = split(rest)
    weight = dot(onehot, w1, TN) + dot(onehot, w2, TN) + dot(onehot, w3, TN)
    mask = lax.broadcasted_iota(jnp.int32, (CH, CH), 0) >= lax.broadcasted_iota(jnp.int32, (CH, CH), 1)

    def before(n):
        lanes = pl.ds(n * D, D)
        scaled[n] = c_ref[:, lanes] * weight
        upper, lower = features(q_ref[:, lanes], qw_ref[n])
        qf[n, :, :D] = upper
        qf[n, :, D:] = lower
        qh[n], ql[n] = split(qf[n])
        qth[n], qtl[n] = split(jnp.transpose(qf[n]))
        for c in range(NC):
            r = pl.ds(c * CH, CH)
            s = mm3((qh[n, r, :], ql[n, r, :]), (kh[r, :], kl[r, :]), NT)
            sh[n, r, :], sl[n, r, :] = split(jnp.where(mask, s, 0.0))
            intra[n, r, :] = mm3((sh[n, r, :], sl[n, r, :]), (vh[r, :], vl[r, :]), NN)

    recv_x(ra.at[:, pl.ds(0, TM)], 0)
    ta[...] = total(ra)
    send_z(lambda zp: ta.at[pl.ds(0, TM)], za.at[:, pl.ds(0, TM)], 0, z + 1, ZN)
    before(0)
    wait_z(za.at[:, pl.ds(0, TM)], r_two, 0, 0, z)
    pre = jnp.sum(za[...], axis=0)
    pre_tot = pre[TR:TM]
    for i in range(XN):
        gas[i] = pre[:TR]
        if i < XN - 1:
            pre = pre + ra[i]
            pre_tot = pre_tot + jnp.where(i < x, ra[i, TR:TM], 0.0)
    send_group(lambda t, xp, hp: gas.at[xp], ga, 1)
    ga[me] = gas[x]
    before(1)
    recv_group(ga, 1)

    p_now = ga[...].reshape(2 * D, D)
    tot_now = (pre_tot[0:1], pre_tot[1:2])
    states, totals = [], []
    for c in range(NC):
        states.append(split(p_now))
        totals.append(tot_now)
        if c < NC - 1:
            p_now = p_now + st[c]
            tot_now = (tot_now[0] + tot[c][0], tot_now[1] + tot[c][1])
    ct = [[0.0, 0.0] for _ in range(NC)]
    carried = []
    for c in range(NC):
        r = pl.ds(c * CH, CH)
        thi, tlo = split(jnp.concatenate([column(totals[c][0]), column(totals[c][1])], axis=0))
        full = (jnp.concatenate([states[c][0], thi], axis=1), jnp.concatenate([states[c][1], tlo], axis=1))
        acc = None
        for n in range(2):
            q = (qh[n, r, :], ql[n, r, :])
            nn = intra[n, r, :] + mm3(q, full, NN)
            inv = 1.0 / nn[:, D:]
            sc = scaled[n, r, :]
            gnum = sc * inv
            gno = -jnp.sum(sc * (nn[:, :D] * inv), axis=1, keepdims=True) * inv
            gnorm[n, r, :] = gno
            g = split(gnum)
            gnh[n, r, :], gnl[n, r, :] = g
            ct[c][0] = ct[c][0] + jnp.sum(gno * qf[n, r, :D], axis=0, keepdims=True)
            ct[c][1] = ct[c][1] + jnp.sum(gno * qf[n, r, D:], axis=0, keepdims=True)
            term = mm3((qth[n, :, r], qtl[n, :, r]), g, NN)
            acc = term if acc is None else acc + term
        carried.append(acc)
    c1[...] = carried[1]
    whole = carried[0] + carried[1]
    ct_all = jnp.concatenate([ct[0][0] + ct[1][0], ct[0][1] + ct[1][1]], axis=0)
    for t in range(GN):
        cb[t, :TR] = whole[TR * t:TR * t + TR]
        cb[t, TR:TM] = ct_all
    send_group(lambda t, xp, hp: cb.at[t, pl.ds(0, TM)], rb.at[:, pl.ds(0, TM)], 2)
    rb[me] = cb[me]

    def after(n):
        lanes = pl.ds(n * D, D)
        wpair = split(qw_ref[n])
        xs = split(q_ref[:, lanes])
        grads = []
        for c in range(NC):
            r = pl.ds(c * CH, CH)
            g = (gnh[n, r, :], gnl[n, r, :])
            gno = gnorm[n, r, :]
            gs = mm3(g, (vh[r, :D], vl[r, :D]), NT) + jnp.concatenate([gno, gno], axis=1)
            gs = split(jnp.where(mask, gs, 0.0))
            gfeat = mm3(gs, (kh[r, :], kl[r, :]), NN) + mm3(g, states[c], NT)
            a = gfeat[:, :D] + gno * totals[c][0]
            b = gfeat[:, D:] + gno * totals[c][1]
            gl = split(back(qf[n, r, :D], qf[n, r, D:], a, b))
            grads.append(gl)
            gq_ref[r, lanes] = mm3(gl, wpair, NT)
            gk = mm3(gs, (qh[n, r, :], ql[n, r, :]), TN)
            gv = mm3((sh[n, r, :], sl[n, r, :]), g, TN)
            if n == 0:
                gkf[r, :] = gk
                gval[r, :] = gv
            else:
                gkf[r, :] += gk
                gval[r, :] += gv
        gl = (jnp.concatenate([g[0] for g in grads], axis=0), jnp.concatenate([g[1] for g in grads], axis=0))
        gw = mm3(xs, gl, TN)
        parts = XN // 2
        for i in range(parts):
            qs[parts * n + i] = gw[QX * i:QX * i + QX]

    after(0)
    after(1)
    stores[0].start()
    recv_group(rb.at[:, pl.ds(0, TM)], 2)
    by_x = []
    for i in range(XN):
        s = rb[i]
        for hp in range(1, HN):
            s = s + rb[hp * XN + i]
        by_x.append(s)
    tb[...] = total(by_x)
    send_z(lambda zp: tb.at[pl.ds(0, TM)], zb.at[:, pl.ds(0, TM)], 1, 0, z)

    r = pl.ds(0, CH)
    cpair = split(c1[...])
    gkf[r, :] += mm3((vh[r, :D], vl[r, :D]), cpair, NT) + jnp.concatenate([ct[1][0], ct[1][1]], axis=1)
    gval[r, :] += mm3((kh[r, :], kl[r, :]), cpair, NN)
    gl = back(kf[:, :D], kf[:, D:], gkf[:, :D], gkf[:, D:])
    for i in range(HN):
        ks[i, :, :D] = gl[OWN * i:OWN * i + OWN]
        ks[i, :, D:] = gval[OWN * i:OWN * i + OWN, :]

    def send_key(i, carry):
        hp = (h + i) % HN
        start(ks.at[hp], kr.at[h], s_one.at[5], r_one.at[5], pos, hp)
        return carry
    lax.fori_loop(1, HN, send_key, 0)
    kr[h] = ks[h]
    kpair = (kth[...], ktl[...])
    gkw = mm3(kpair, split(gl), NN)
    for i in range(GN):
        iks[i] = gkw[KW * i:KW * i + KW]
    send_group(lambda t, xp, hp: iks.at[t], ikr, 9)
    ikr[me] = iks[me]
    send_x(lambda xp: qs.at[xp], rq, 3)
    rq[x] = qs[x]

    wait_z(zb.at[:, pl.ds(0, TM)], r_two, 1, z + 1, ZN)
    suf = jnp.sum(zb[...], axis=0)
    suf_tot = suf[TR:TM]
    for i in reversed(range(XN)):
        gbs[i] = suf[:TR]
        if i > 0:
            suf = suf + by_x[i]
            suf_tot = suf_tot + jnp.where(i > x, by_x[i][TR:TM], 0.0)
    send_group(lambda t, xp, hp: gbs.at[xp], gb, 4)
    gb[me] = gbs[x]

    recv_x(rq, 3)
    tsum = total(rq)
    for i in range(ZN):
        tq[i] = tsum[QZ * i:QZ * i + QZ]
    send_z(lambda zp: tq.at[zp], zq, 2, 0, ZN)
    zq[z] = tq[z]
    recv_group(ikr, 9)
    early = jnp.sum(ikr[...], axis=0)

    recv_group(gb, 4)
    later = split(gb[...].reshape(2 * D, D))
    gfeat = mm3((vh[:, :D], vl[:, :D]), later, NT)
    gl = back(kf[:, :D], kf[:, D:], gfeat[:, :D] + suf_tot[0:1], gfeat[:, D:] + suf_tot[1:2])
    gkw = mm3(kpair, split(gl), NN)
    for i in range(GN):
        ck[i] = gkw[KW * i:KW * i + KW]
    send_x(lambda xp: ck.at[h * XN + xp], rc, 6)
    rc[x] = ck[me]
    gint[...] = gl

    own = pl.ds(h * OWN, OWN)
    drain(kr.at[pl.ds(0, HN - 1)], r_one.at[5])
    got = kr[0]
    for i in range(1, HN):
        got = got + kr[i]
    gk_ref[...] = mm3(split(gint[own, :] + got[:, :D]), split(kw_ref[...]), NT)
    gv_ref[...] = mm3((kh[own, :], kl[own, :]), later, NN) + got[:, D:]

    stores[1].start()
    stores[2].start()

    recv_x(rc, 6)
    tc[...] = total(rc) + early
    send_z(lambda zp: tc, zc, 4, 0, ZN)
    zc[z] = tc[...]

    wait_z(zq, r_two, 2, 0, ZN)
    gzs[...] = jnp.sum(zq[...], axis=0)
    send_z(lambda zp: gzs, gz, 3, 0, ZN)
    gz[z] = gzs[...]

    wait_z(zc, r_two, 4, 0, ZN)
    gcs[...] = jnp.sum(zc[...], axis=0)
    send_group(lambda t, xp, hp: gcs, gc, 8)
    gc[me] = gcs[...]

    wait_z(gz, r_two, 3, 0, ZN)
    send_x(lambda xp: gz, gx, 7)
    gx[x] = gz[...]

    recv_x(gx, 7)
    for i in range(XN):
        for j in range(ZN):
            row = QX * i + QZ * j
            gqw_ref[row // D, row % D:row % D + QZ, :] = gx[i, j]
    stores[3].start()
    recv_group(gc, 8)
    for i in range(GN):
        gkw_ref[KW * i:KW * i + KW, :] = gc[i]
    stores[4].start()

    sent_x(ra.at[:, pl.ds(0, TM)], 0)
    sent_group(ga, 1)
    sent_group(rb.at[:, pl.ds(0, TM)], 2)
    sent_x(rq, 3)
    sent_group(gb, 4)
    drain(kr.at[pl.ds(0, HN - 1)], s_one.at[5])
    sent_x(rc, 6)
    sent_group(ikr, 9)
    sent_x(gx, 7)
    sent_group(gc, 8)
    wait_z(za.at[:, pl.ds(0, TM)], s_two, 0, z + 1, ZN)
    wait_z(zb.at[:, pl.ds(0, TM)], s_two, 1, 0, z)
    wait_z(zq, s_two, 2, 0, ZN)
    wait_z(gz, s_two, 3, 0, ZN)
    wait_z(zc, s_two, 4, 0, ZN)
    for copy in stores:
        copy.wait()


def store(*refs):
    sems = refs[10]
    copies = [pltpu.make_async_copy(refs[i], refs[5 + i], sems.at[i]) for i in range(5)]
    for copy in copies:
        copy.start()
    for copy in copies:
        copy.wait()


def on_device(queries, keys, values, cotangent, source_ids, source_weights, q_feature, k_feature):
    def vm(*shape, dtype=F32):
        return pltpu.VMEM(shape, dtype)

    b = dict(dtype=BF16)
    results = pl.pallas_call(
        kernel,
        out_shape=(
            jax.ShapeDtypeStruct((ROWS, 2 * D), F32),
            jax.ShapeDtypeStruct((OWN, D), F32),
            jax.ShapeDtypeStruct((OWN, D), F32),
            jax.ShapeDtypeStruct((2, D, D), F32),
            jax.ShapeDtypeStruct((D, D), F32),
        ),
        in_specs=[pl.BlockSpec(memory_space=pl.ANY)] * 8,
        out_specs=[pl.BlockSpec(memory_space=pl.ANY)] * 5,
        scratch_shapes=[
            vm(ROWS, 2 * D), vm(OWN, D), vm(OWN, D), vm(2, D, D), vm(D, D), pltpu.SemaphoreType.DMA((5,)),
            vm(ROWS, 2 * D), vm(ROWS, D), vm(ROWS, D), vm(ROWS, 2 * D), vm(1, ROWS, dtype=jnp.int32), vm(1, 64),
            vm(2, D, D), vm(D, D), pltpu.SemaphoreType.DMA((8,)),
            vm(ROWS, 2 * D), vm(ROWS, 2 * D, **b), vm(ROWS, 2 * D, **b),
            vm(ROWS, 2 * D, **b), vm(ROWS, 2 * D, **b),
            vm(2, ROWS, 2 * D), vm(2, ROWS, 2 * D, **b), vm(2, ROWS, 2 * D, **b),
            vm(2, ROWS, CH, **b), vm(2, ROWS, CH, **b),
            vm(2, ROWS, 2 * D), vm(2, ROWS, D), vm(NC, 2 * D, D),
            vm(2, ROWS, D, **b), vm(2, ROWS, D, **b), vm(2, ROWS, D),
            vm(2 * D, D), vm(ROWS, 2 * D), vm(ROWS, D),
            vm(XN, TP, D), vm(XN, TP, D), vm(TP, D), vm(ZN, TP, D), vm(XN, TR, D), vm(GN, TR, D),
            vm(GN, TP, D), vm(GN, TP, D), vm(TP, D), vm(ZN, TP, D), vm(XN, TR, D), vm(GN, TR, D),
            vm(HN, OWN, 2 * D), vm(HN, OWN, 2 * D),
            vm(XN, QX, D), vm(XN, QX, D), vm(ZN, QZ, D), vm(ZN, QZ, D),
            vm(QZ, D), vm(ZN, QZ, D), vm(XN, ZN, QZ, D),
            vm(GN, KW, D), vm(XN, KW, D), vm(KW, D), vm(ZN, KW, D), vm(KW, D), vm(GN, KW, D),
            vm(2, 2 * D, ROWS, **b), vm(2, 2 * D, ROWS, **b), vm(D, ROWS, **b), vm(D, ROWS, **b),
            vm(GN, KW, D), vm(GN, KW, D), vm(ROWS, D),
            pltpu.SemaphoreType.DMA((10,)),
            pltpu.SemaphoreType.DMA((5, ZN)),
            pltpu.SemaphoreType.DMA((10,)),
            pltpu.SemaphoreType.DMA((5, ZN)),
        ],
        compiler_params=pltpu.CompilerParams(
            collective_id=0, has_side_effects=True, vmem_limit_bytes=60 * 1024 * 1024
        ),
        cost_estimate=pl.CostEstimate(flops=3_000_000_000, bytes_accessed=2_500_000, transcendentals=400_000),
    )(queries, keys, values, cotangent, source_ids.reshape(1, ROWS), source_weights.reshape(1, -1), q_feature, k_feature)
    return pl.pallas_call(
        store,
        out_shape=[jax.ShapeDtypeStruct(a.shape, a.dtype) for a in results],
        in_specs=[pl.BlockSpec(memory_space=pl.ANY)] * 5,
        out_specs=[pl.BlockSpec(memory_space=pl.ANY)] * 5,
        scratch_shapes=[pltpu.SemaphoreType.DMA((5,))],
    )(*results)


def solution(mesh):
    placed = (
        P("ctx", "head"),
        P("ctx", None),
        P("ctx", None),
        P("ctx", "head"),
        P("ctx"),
        P(),
        P("head", None, None),
        P(),
    )
    return jax.shard_map(
        on_device,
        mesh=mesh,
        in_specs=placed,
        out_specs=(
            P("ctx", "head"),
            P(("ctx", "head"), None),
            P(("ctx", "head"), None),
            P("head", None, None),
            P(),
        ),
        check_vma=False,
    )
```

```python
import jax
import jax.numpy as jnp
from jax import lax
from jax.experimental import pallas as pl
from jax.experimental.pallas import tpu as pltpu
from jax.sharding import PartitionSpec as P

MESH = pl.DeviceIdType.MESH
F32 = jnp.float32
BF16 = jnp.bfloat16
NN = ((1,), (0,))
NT = ((1,), (1,))
TN = ((0,), (0,))
XN = 4
ZN = 16
HN = 8
GN = XN * HN
ROWS = 512
CH = 256
D = 128
NC = ROWS // CH
OWN = ROWS // HN
TR = 2 * D // GN
TM = TR + 2
TP = TR + 8
KW = D // GN
QX = 2 * D // XN
QZ = QX // ZN


def split(a):
    high = a.astype(BF16)
    return high, (a - high.astype(F32)).astype(BF16)


def dot(a, b, dims):
    return lax.dot_general(a, b, (dims, ((), ())), preferred_element_type=F32)


def mm3(a, b, dims):
    (ah, al), (bh, bl) = a, b
    return dot(ah, bh, dims) + (dot(ah, bl, dims) + dot(al, bh, dims))


def total(parts):
    acc = parts[0]
    for i in range(1, XN):
        acc = acc + parts[i]
    return acc


def features(inputs, weight):
    logits = jnp.dot(inputs, weight, precision=lax.Precision.HIGHEST, preferred_element_type=F32)
    upper = jnp.exp(logits - jnp.max(logits, axis=1, keepdims=True))
    lower = jnp.exp(jnp.min(logits, axis=1, keepdims=True) - logits)
    upper = upper * (1.0 / jnp.sum(upper, axis=1, keepdims=True))
    lower = lower * (1.0 / jnp.sum(lower, axis=1, keepdims=True))
    return upper, lower


def back(upper, lower, a, b):
    up = upper * (a - jnp.sum(upper * a, axis=1, keepdims=True))
    return up - lower * (b - jnp.sum(lower * b, axis=1, keepdims=True))


def column(row):
    return jnp.transpose(jnp.broadcast_to(row, (D, D)))


def swing(i, n):
    return (n // 2 + ((i + 1) // 2) * (1 - 2 * (i % 2))) % n


def kernel(
    q_in, k_in, v_in, c_in, ids_in, sw_in, qw_in, kw_in,
    gq_out, gk_out, gv_out, gqw_out, gkw_out,
    gq_ref, gk_ref, gv_ref, gqw_ref, gkw_ref, o_sem,
    q_ref, k_ref, v_ref, c_ref, ids_ref, sw_ref, qw_ref, kw_ref, i_sem,
    kf, kh, kl, vh, vl, qf, qh, ql, sh, sl, intra, scaled, st, gnh, gnl, gnorm, c1, gkf, gval,
    sa, ra, ta, za, gas, ga, cb, rb, tb, zb, gbs, gb, ks, kr, qs, rq, tq, zq, gzs, gz, gx, ck, rc, tc, zc, gcs, gc,
    qth, qtl, kth, ktl, iks, ikr, gint,
    s_one, s_two, r_one, r_two,
):
    pos = lax.axis_index("ctx")
    h = lax.axis_index("head")
    z = pos // XN
    x = pos % XN
    me = h * XN + x

    def each_group(act):
        def step(i, carry):
            xp = (x + swing(i // HN, XN)) % XN
            yp = (h // 2 + swing(i // 2 % (HN // 2), HN // 2)) % (HN // 2)
            hp = yp * 2 + (h + i + 1) % 2
            act(hp * XN + xp, xp, hp)
            return carry
        lax.fori_loop(0, GN - 1, step, 0)

    def each_z(act):
        def step(i, carry):
            act((z + swing(i, ZN)) % ZN)
            return carry
        lax.fori_loop(0, ZN - 1, step, 0)

    barrier = pltpu.get_barrier_semaphore()

    def greet(ctx, head):
        pl.semaphore_signal(barrier, inc=1, device_id=(ctx, head), device_id_type=MESH)

    loads = [
        pltpu.make_async_copy(src, dst, i_sem.at[i])
        for i, (src, dst) in enumerate([
            (k_in, k_ref), (kw_in, kw_ref), (v_in, v_ref), (q_in, q_ref),
            (qw_in, qw_ref), (c_in, c_ref), (ids_in, ids_ref), (sw_in, sw_ref),
        ])
    ]
    for load in loads:
        load.start()
    stores = [
        pltpu.make_async_copy(src, dst, o_sem.at[i])
        for i, (src, dst) in enumerate([
            (gq_ref, gq_out), (gk_ref, gk_out), (gv_ref, gv_out), (gqw_ref, gqw_out), (gkw_ref, gkw_out),
        ])
    ]
    za[...] = jnp.zeros_like(za)
    zb[...] = jnp.zeros_like(zb)
    each_z(lambda zp: greet(zp * XN + x, h))
    each_group(lambda t, xp, hp: greet(z * XN + xp, hp))

    pend = []

    def finish():
        for act in pend:
            act()

    def start(src, dst, ssem, rsem, ctx, head):
        pltpu.make_async_remote_copy(
            src_ref=src, dst_ref=dst, send_sem=ssem, recv_sem=rsem,
            device_id=(ctx, head), device_id_type=MESH,
        ).start()

    def drain(ref, sem):
        pltpu.make_async_copy(ref, ref, sem).wait()

    def send_group(src_of, dst, index):
        each_group(lambda t, xp, hp: start(
            src_of(t, xp, hp), dst.at[me], s_one.at[index], r_one.at[index], z * XN + xp, hp))
        pend.append(lambda: drain(dst.at[pl.ds(0, GN - 1)], s_one.at[index]))

    def recv_group(dst, index):
        drain(dst.at[pl.ds(0, GN - 1)], r_one.at[index])

    def send_x(src_of, dst, index):
        def step(i, carry):
            xp = (x + swing(i, XN)) % XN
            start(src_of(xp), dst.at[x], s_one.at[index], r_one.at[index], z * XN + xp, h)
            return carry
        lax.fori_loop(0, XN - 1, step, 0)
        pend.append(lambda: drain(dst.at[pl.ds(0, XN - 1)], s_one.at[index]))

    def recv_x(dst, index):
        drain(dst.at[pl.ds(0, XN - 1)], r_one.at[index])

    def send_z(src_of, dst, index, low, high):
        def act(zp):
            @pl.when((zp >= low) & (zp < high))
            def _():
                start(src_of(zp), dst.at[z], s_two.at[index, zp], r_two.at[index, z], zp * XN + x, h)
        each_z(act)
        pend.append(lambda: wait_z(dst, s_two, index, low, high))

    def wait_z(dst, sems, index, low, high):
        def step(zp, carry):
            @pl.when(zp != z)
            def _():
                drain(dst.at[zp], sems.at[index, zp])
            return carry
        lax.fori_loop(low, high, step, 0)

    loads[0].wait()
    loads[1].wait()
    upper, lower = features(k_ref[...], kw_ref[...])
    kf[:, :D] = upper
    kf[:, D:] = lower
    kh[...], kl[...] = split(kf[...])
    loads[2].wait()
    vh[:, :D], vl[:, :D] = split(v_ref[...])
    vh[:, D:] = jnp.ones((ROWS, D), BF16)
    vl[:, D:] = jnp.zeros((ROWS, D), BF16)
    tot = []
    for c in range(NC):
        r = pl.ds(c * CH, CH)
        st[c] = mm3((kh[r, :], kl[r, :]), (vh[r, :D], vl[r, :D]), TN)
        tot.append((jnp.sum(kf[r, :D], axis=0, keepdims=True), jnp.sum(kf[r, D:], axis=0, keepdims=True)))
    tot_all = jnp.concatenate([tot[0][0] + tot[1][0], tot[0][1] + tot[1][1]], axis=0)
    mine = st[0, pl.ds(h * (XN * TR), XN * TR), :] + st[1, pl.ds(h * (XN * TR), XN * TR), :]
    for i in range(XN):
        sa[i, :TR] = mine[TR * i:TR * i + TR]
        sa[i, TR:TM] = tot_all
    pl.semaphore_wait(barrier, GN - 1 + ZN - 1)
    send_x(lambda xp: sa.at[xp, pl.ds(0, TM)], ra.at[:, pl.ds(0, TM)], 0)
    ra[x] = sa[x]

    for load in loads[3:]:
        load.wait()
    kth[...], ktl[...] = split(jnp.transpose(k_ref[...]))

    ids = ids_ref[...]
    onehot = (lax.broadcasted_iota(jnp.int32, (64, ROWS), 0) == ids).astype(F32).astype(BF16)
    diag = lax.broadcasted_iota(jnp.int32, (64, 64), 0) == lax.broadcasted_iota(jnp.int32, (64, 64), 1)
    wcol = jnp.sum(jnp.where(diag, sw_ref[...], 0.0), axis=1, keepdims=True)
    wtab = jnp.broadcast_to(wcol, (64, D))
    w1, rest = wtab.astype(BF16), wtab - wtab.astype(BF16).astype(F32)
    w2, w3 = split(rest)
    weight = dot(onehot, w1, TN) + dot(onehot, w2, TN) + dot(onehot, w3, TN)
    mask = lax.broadcasted_iota(jnp.int32, (CH, CH), 0) >= lax.broadcasted_iota(jnp.int32, (CH, CH), 1)

    def before(n):
        lanes = pl.ds(n * D, D)
        scaled[n] = c_ref[:, lanes] * weight
        upper, lower = features(q_ref[:, lanes], qw_ref[n])
        qf[n, :, :D] = upper
        qf[n, :, D:] = lower
        qh[n], ql[n] = split(qf[n])
        qth[n], qtl[n] = split(jnp.transpose(qf[n]))
        for c in range(NC):
            r = pl.ds(c * CH, CH)
            s = mm3((qh[n, r, :], ql[n, r, :]), (kh[r, :], kl[r, :]), NT)
            sh[n, r, :], sl[n, r, :] = split(jnp.where(mask, s, 0.0))
            intra[n, r, :] = mm3((sh[n, r, :], sl[n, r, :]), (vh[r, :], vl[r, :]), NN)

    recv_x(ra.at[:, pl.ds(0, TM)], 0)
    ta[...] = total(ra)
    send_z(lambda zp: ta.at[pl.ds(0, TM)], za.at[:, pl.ds(0, TM)], 0, z + 1, ZN)
    before(0)
    wait_z(za.at[:, pl.ds(0, TM)], r_two, 0, 0, z)
    pre = jnp.sum(za[...], axis=0)
    pre_tot = pre[TR:TM]
    for i in range(XN):
        gas[i] = pre[:TR]
        if i < XN - 1:
            pre = pre + ra[i]
            pre_tot = pre_tot + jnp.where(i < x, ra[i, TR:TM], 0.0)
    send_group(lambda t, xp, hp: gas.at[xp], ga, 1)
    ga[me] = gas[x]
    before(1)
    recv_group(ga, 1)

    p_now = ga[...].reshape(2 * D, D)
    tot_now = (pre_tot[0:1], pre_tot[1:2])
    states, totals = [], []
    for c in range(NC):
        states.append(split(p_now))
        totals.append(tot_now)
        if c < NC - 1:
            p_now = p_now + st[c]
            tot_now = (tot_now[0] + tot[c][0], tot_now[1] + tot[c][1])
    ct = [[0.0, 0.0] for _ in range(NC)]
    carried = []
    for c in range(NC):
        r = pl.ds(c * CH, CH)
        thi, tlo = split(jnp.concatenate([column(totals[c][0]), column(totals[c][1])], axis=0))
        full = (jnp.concatenate([states[c][0], thi], axis=1), jnp.concatenate([states[c][1], tlo], axis=1))
        acc = None
        for n in range(2):
            q = (qh[n, r, :], ql[n, r, :])
            nn = intra[n, r, :] + mm3(q, full, NN)
            inv = 1.0 / nn[:, D:]
            sc = scaled[n, r, :]
            gnum = sc * inv
            gno = -jnp.sum(sc * (nn[:, :D] * inv), axis=1, keepdims=True) * inv
            gnorm[n, r, :] = gno
            g = split(gnum)
            gnh[n, r, :], gnl[n, r, :] = g
            ct[c][0] = ct[c][0] + jnp.sum(gno * qf[n, r, :D], axis=0, keepdims=True)
            ct[c][1] = ct[c][1] + jnp.sum(gno * qf[n, r, D:], axis=0, keepdims=True)
            term = mm3((qth[n, :, r], qtl[n, :, r]), g, NN)
            acc = term if acc is None else acc + term
        carried.append(acc)
    c1[...] = carried[1]
    whole = carried[0] + carried[1]
    ct_all = jnp.concatenate([ct[0][0] + ct[1][0], ct[0][1] + ct[1][1]], axis=0)
    for t in range(GN):
        cb[t, :TR] = whole[TR * t:TR * t + TR]
        cb[t, TR:TM] = ct_all
    send_group(lambda t, xp, hp: cb.at[t, pl.ds(0, TM)], rb.at[:, pl.ds(0, TM)], 2)
    rb[me] = cb[me]

    def after(n):
        lanes = pl.ds(n * D, D)
        wpair = split(qw_ref[n])
        xs = split(q_ref[:, lanes])
        grads = []
        for c in range(NC):
            r = pl.ds(c * CH, CH)
            g = (gnh[n, r, :], gnl[n, r, :])
            gno = gnorm[n, r, :]
            gs = mm3(g, (vh[r, :D], vl[r, :D]), NT) + jnp.concatenate([gno, gno], axis=1)
            gs = split(jnp.where(mask, gs, 0.0))
            gfeat = mm3(gs, (kh[r, :], kl[r, :]), NN) + mm3(g, states[c], NT)
            a = gfeat[:, :D] + gno * totals[c][0]
            b = gfeat[:, D:] + gno * totals[c][1]
            gl = split(back(qf[n, r, :D], qf[n, r, D:], a, b))
            grads.append(gl)
            gq_ref[r, lanes] = mm3(gl, wpair, NT)
            gk = mm3(gs, (qh[n, r, :], ql[n, r, :]), TN)
            gv = mm3((sh[n, r, :], sl[n, r, :]), g, TN)
            if n == 0:
                gkf[r, :] = gk
                gval[r, :] = gv
            else:
                gkf[r, :] += gk
                gval[r, :] += gv
        gl = (jnp.concatenate([g[0] for g in grads], axis=0), jnp.concatenate([g[1] for g in grads], axis=0))
        gw = mm3(xs, gl, TN)
        parts = XN // 2
        for i in range(parts):
            qs[parts * n + i] = gw[QX * i:QX * i + QX]

    after(0)
    after(1)
    stores[0].start()
    recv_group(rb.at[:, pl.ds(0, TM)], 2)
    by_x = []
    for i in range(XN):
        s = rb[i]
        for hp in range(1, HN):
            s = s + rb[hp * XN + i]
        by_x.append(s)
    tb[...] = total(by_x)
    send_z(lambda zp: tb.at[pl.ds(0, TM)], zb.at[:, pl.ds(0, TM)], 1, 0, z)

    r = pl.ds(0, CH)
    cpair = split(c1[...])
    gkf[r, :] += mm3((vh[r, :D], vl[r, :D]), cpair, NT) + jnp.concatenate([ct[1][0], ct[1][1]], axis=1)
    gval[r, :] += mm3((kh[r, :], kl[r, :]), cpair, NN)
    gl = back(kf[:, :D], kf[:, D:], gkf[:, :D], gkf[:, D:])
    for i in range(HN):
        ks[i, :, :D] = gl[OWN * i:OWN * i + OWN]
        ks[i, :, D:] = gval[OWN * i:OWN * i + OWN, :]

    def send_key(i, carry):
        hp = (h + i) % HN
        start(ks.at[hp], kr.at[h], s_one.at[5], r_one.at[5], pos, hp)
        return carry
    lax.fori_loop(1, HN, send_key, 0)
    pend.append(lambda: drain(kr.at[pl.ds(0, HN - 1)], s_one.at[5]))
    kr[h] = ks[h]
    kpair = (kth[...], ktl[...])
    gkw = mm3(kpair, split(gl), NN)
    for i in range(GN):
        iks[i] = gkw[KW * i:KW * i + KW]
    send_group(lambda t, xp, hp: iks.at[t], ikr, 9)
    ikr[me] = iks[me]
    send_x(lambda xp: qs.at[xp], rq, 3)
    rq[x] = qs[x]

    wait_z(zb.at[:, pl.ds(0, TM)], r_two, 1, z + 1, ZN)
    suf = jnp.sum(zb[...], axis=0)
    suf_tot = suf[TR:TM]
    for i in reversed(range(XN)):
        gbs[i] = suf[:TR]
        if i > 0:
            suf = suf + by_x[i]
            suf_tot = suf_tot + jnp.where(i > x, by_x[i][TR:TM], 0.0)
    send_group(lambda t, xp, hp: gbs.at[xp], gb, 4)
    gb[me] = gbs[x]

    recv_x(rq, 3)
    tsum = total(rq)
    for i in range(ZN):
        tq[i] = tsum[QZ * i:QZ * i + QZ]
    send_z(lambda zp: tq.at[zp], zq, 2, 0, ZN)
    zq[z] = tq[z]
    recv_group(ikr, 9)
    early = jnp.sum(ikr[...], axis=0)

    recv_group(gb, 4)
    later = split(gb[...].reshape(2 * D, D))
    gfeat = mm3((vh[:, :D], vl[:, :D]), later, NT)
    gl = back(kf[:, :D], kf[:, D:], gfeat[:, :D] + suf_tot[0:1], gfeat[:, D:] + suf_tot[1:2])
    gkw = mm3(kpair, split(gl), NN)
    for i in range(GN):
        ck[i] = gkw[KW * i:KW * i + KW]
    send_x(lambda xp: ck.at[h * XN + xp], rc, 6)
    rc[x] = ck[me]
    gint[...] = gl

    own = pl.ds(h * OWN, OWN)
    drain(kr.at[pl.ds(0, HN - 1)], r_one.at[5])
    got = kr[0]
    for i in range(1, HN):
        got = got + kr[i]
    gk_ref[...] = mm3(split(gint[own, :] + got[:, :D]), split(kw_ref[...]), NT)
    gv_ref[...] = mm3((kh[own, :], kl[own, :]), later, NN) + got[:, D:]

    stores[1].start()
    stores[2].start()

    recv_x(rc, 6)
    tc[...] = total(rc) + early
    send_z(lambda zp: tc, zc, 4, 0, ZN)
    zc[z] = tc[...]

    wait_z(zq, r_two, 2, 0, ZN)
    gzs[...] = jnp.sum(zq[...], axis=0)
    send_z(lambda zp: gzs, gz, 3, 0, ZN)
    gz[z] = gzs[...]

    wait_z(zc, r_two, 4, 0, ZN)
    gcs[...] = jnp.sum(zc[...], axis=0)
    send_group(lambda t, xp, hp: gcs, gc, 8)
    gc[me] = gcs[...]

    wait_z(gz, r_two, 3, 0, ZN)
    send_x(lambda xp: gz, gx, 7)
    gx[x] = gz[...]

    recv_x(gx, 7)
    for i in range(XN):
        for j in range(ZN):
            row = QX * i + QZ * j
            gqw_ref[row // D, row % D:row % D + QZ, :] = gx[i, j]
    stores[3].start()
    recv_group(gc, 8)
    for i in range(GN):
        gkw_ref[KW * i:KW * i + KW, :] = gc[i]
    stores[4].start()

    for copy in stores:
        copy.wait()
    finish()


def store(*refs):
    sources, targets, held, sems = refs[:5], refs[5:10], refs[10:15], refs[15]
    reads = [pltpu.make_async_copy(sources[i], held[i], sems.at[0, i]) for i in range(5)]
    writes = [pltpu.make_async_copy(held[i], targets[i], sems.at[1, i]) for i in range(5)]
    for read in reads:
        read.start()
    for read, write in zip(reads, writes):
        read.wait()
        write.start()
    for write in writes:
        write.wait()


def on_device(queries, keys, values, cotangent, source_ids, source_weights, q_feature, k_feature):
    def vm(*shape, dtype=F32):
        return pltpu.VMEM(shape, dtype)

    b = dict(dtype=BF16)
    results = pl.pallas_call(
        kernel,
        out_shape=(
            jax.ShapeDtypeStruct((ROWS, 2 * D), F32),
            jax.ShapeDtypeStruct((OWN, D), F32),
            jax.ShapeDtypeStruct((OWN, D), F32),
            jax.ShapeDtypeStruct((2, D, D), F32),
            jax.ShapeDtypeStruct((D, D), F32),
        ),
        in_specs=[pl.BlockSpec(memory_space=pl.ANY)] * 8,
        out_specs=[pl.BlockSpec(memory_space=pl.ANY)] * 5,
        scratch_shapes=[
            vm(ROWS, 2 * D), vm(OWN, D), vm(OWN, D), vm(2, D, D), vm(D, D), pltpu.SemaphoreType.DMA((5,)),
            vm(ROWS, 2 * D), vm(ROWS, D), vm(ROWS, D), vm(ROWS, 2 * D), vm(1, ROWS, dtype=jnp.int32), vm(1, 64),
            vm(2, D, D), vm(D, D), pltpu.SemaphoreType.DMA((8,)),
            vm(ROWS, 2 * D), vm(ROWS, 2 * D, **b), vm(ROWS, 2 * D, **b),
            vm(ROWS, 2 * D, **b), vm(ROWS, 2 * D, **b),
            vm(2, ROWS, 2 * D), vm(2, ROWS, 2 * D, **b), vm(2, ROWS, 2 * D, **b),
            vm(2, ROWS, CH, **b), vm(2, ROWS, CH, **b),
            vm(2, ROWS, 2 * D), vm(2, ROWS, D), vm(NC, 2 * D, D),
            vm(2, ROWS, D, **b), vm(2, ROWS, D, **b), vm(2, ROWS, D),
            vm(2 * D, D), vm(ROWS, 2 * D), vm(ROWS, D),
            vm(XN, TP, D), vm(XN, TP, D), vm(TP, D), vm(ZN, TP, D), vm(XN, TR, D), vm(GN, TR, D),
            vm(GN, TP, D), vm(GN, TP, D), vm(TP, D), vm(ZN, TP, D), vm(XN, TR, D), vm(GN, TR, D),
            vm(HN, OWN, 2 * D), vm(HN, OWN, 2 * D),
            vm(XN, QX, D), vm(XN, QX, D), vm(ZN, QZ, D), vm(ZN, QZ, D),
            vm(QZ, D), vm(ZN, QZ, D), vm(XN, ZN, QZ, D),
            vm(GN, KW, D), vm(XN, KW, D), vm(KW, D), vm(ZN, KW, D), vm(KW, D), vm(GN, KW, D),
            vm(2, 2 * D, ROWS, **b), vm(2, 2 * D, ROWS, **b), vm(D, ROWS, **b), vm(D, ROWS, **b),
            vm(GN, KW, D), vm(GN, KW, D), vm(ROWS, D),
            pltpu.SemaphoreType.DMA((10,)),
            pltpu.SemaphoreType.DMA((5, ZN)),
            pltpu.SemaphoreType.DMA((10,)),
            pltpu.SemaphoreType.DMA((5, ZN)),
        ],
        compiler_params=pltpu.CompilerParams(
            collective_id=0, has_side_effects=True, vmem_limit_bytes=60 * 1024 * 1024
        ),
        cost_estimate=pl.CostEstimate(flops=3_000_000_000, bytes_accessed=2_500_000, transcendentals=400_000),
    )(queries, keys, values, cotangent, source_ids.reshape(1, ROWS), source_weights.reshape(1, -1), q_feature, k_feature)
    return pl.pallas_call(
        store,
        out_shape=[jax.ShapeDtypeStruct(a.shape, a.dtype) for a in results],
        in_specs=[pl.BlockSpec(memory_space=pl.ANY)] * 5,
        out_specs=[pl.BlockSpec(memory_space=pl.ANY)] * 5,
        scratch_shapes=[pltpu.VMEM(a.shape, a.dtype) for a in results] + [pltpu.SemaphoreType.DMA((2, 5))],
        compiler_params=pltpu.CompilerParams(vmem_limit_bytes=60 * 1024 * 1024),
    )(*results)


def solution(mesh):
    placed = (
        P("ctx", "head"),
        P("ctx", None),
        P("ctx", None),
        P("ctx", "head"),
        P("ctx"),
        P(),
        P("head", None, None),
        P(),
    )
    return jax.shard_map(
        on_device,
        mesh=mesh,
        in_specs=placed,
        out_specs=(
            P("ctx", "head"),
            P(("ctx", "head"), None),
            P(("ctx", "head"), None),
            P("head", None, None),
            P(),
        ),
        check_vma=False,
    )
```

```python
import jax
import jax.numpy as jnp
from jax import lax
from jax.experimental import pallas as pl
from jax.experimental.pallas import tpu as pltpu
from jax.sharding import PartitionSpec as P

MESH = pl.DeviceIdType.MESH
F32 = jnp.float32
BF16 = jnp.bfloat16
NN = ((1,), (0,))
NT = ((1,), (1,))
TN = ((0,), (0,))
XN = 4
ZN = 16
HN = 8
GN = XN * HN
ROWS = 512
CH = 256
D = 128
NC = ROWS // CH
OWN = ROWS // HN
TR = 2 * D // GN
TM = TR + 2
TP = TR + 8
KW = D // GN
QX = 2 * D // XN
QZ = QX // ZN


def split(a):
    high = a.astype(BF16)
    return high, (a - high.astype(F32)).astype(BF16)


def dot(a, b, dims):
    return lax.dot_general(a, b, (dims, ((), ())), preferred_element_type=F32)


def mm3(a, b, dims):
    (ah, al), (bh, bl) = a, b
    return dot(ah, bh, dims) + (dot(ah, bl, dims) + dot(al, bh, dims))


def total(parts):
    acc = parts[0]
    for i in range(1, XN):
        acc = acc + parts[i]
    return acc


def features(inputs, weight):
    logits = jnp.dot(inputs, weight, precision=lax.Precision.HIGHEST, preferred_element_type=F32)
    upper = jnp.exp(logits - jnp.max(logits, axis=1, keepdims=True))
    lower = jnp.exp(jnp.min(logits, axis=1, keepdims=True) - logits)
    upper = upper * (1.0 / jnp.sum(upper, axis=1, keepdims=True))
    lower = lower * (1.0 / jnp.sum(lower, axis=1, keepdims=True))
    return upper, lower


def back(upper, lower, a, b):
    up = upper * (a - jnp.sum(upper * a, axis=1, keepdims=True))
    return up - lower * (b - jnp.sum(lower * b, axis=1, keepdims=True))


def column(row):
    return jnp.transpose(jnp.broadcast_to(row, (D, D)))


def swing(i, n):
    return (n // 2 + ((i + 1) // 2) * (1 - 2 * (i % 2))) % n


def kernel(
    q_in, k_in, v_in, c_in, ids_in, sw_in, qw_in, kw_in,
    gq_out, gk_out, gv_out, gqw_out, gkw_out,
    gq_ref, gk_ref, gv_ref, gqw_ref, gkw_ref, o_sem,
    q_ref, k_ref, v_ref, c_ref, ids_ref, sw_ref, qw_ref, kw_ref, i_sem,
    kf, kh, kl, vh, vl, qf, qh, ql, sh, sl, intra, scaled, st, gnh, gnl, gnorm, c1, gkf, gval,
    sa, ra, ta, za, gas, ga, cb, rb, tb, zb, gbs, gb, ks, kr, qs, rq, tq, zq, gzs, gz, gx, ck, rc, tc, zc, gcs, gc,
    qth, qtl, kth, ktl, iks, ikr, gint,
    s_one, s_two, r_one, r_two,
):
    pos = lax.axis_index("ctx")
    h = lax.axis_index("head")
    z = pos // XN
    x = pos % XN
    me = h * XN + x

    def each_group(act):
        def step(i, carry):
            xp = (x + swing(i // HN, XN)) % XN
            yp = (h // 2 + swing(i // 2 % (HN // 2), HN // 2)) % (HN // 2)
            hp = yp * 2 + (h + i + 1) % 2
            act(hp * XN + xp, xp, hp)
            return carry
        lax.fori_loop(0, GN - 1, step, 0)

    def each_z(act):
        def step(i, carry):
            act((z + swing(i, ZN)) % ZN)
            return carry
        lax.fori_loop(0, ZN - 1, step, 0)

    barrier = pltpu.get_barrier_semaphore()

    def greet(ctx, head):
        pl.semaphore_signal(barrier, inc=1, device_id=(ctx, head), device_id_type=MESH)

    loads = [
        pltpu.make_async_copy(src, dst, i_sem.at[i])
        for i, (src, dst) in enumerate([
            (k_in, k_ref), (kw_in, kw_ref), (v_in, v_ref), (q_in, q_ref),
            (qw_in, qw_ref), (c_in, c_ref), (ids_in, ids_ref), (sw_in, sw_ref),
        ])
    ]
    for load in loads:
        load.start()
    stores = [
        pltpu.make_async_copy(src, dst, o_sem.at[i])
        for i, (src, dst) in enumerate([
            (gq_ref, gq_out), (gk_ref, gk_out), (gv_ref, gv_out), (gqw_ref, gqw_out), (gkw_ref, gkw_out),
        ])
    ]
    za[...] = jnp.zeros_like(za)
    zb[...] = jnp.zeros_like(zb)
    each_z(lambda zp: greet(zp * XN + x, h))
    each_group(lambda t, xp, hp: greet(z * XN + xp, hp))

    pend = []

    def finish():
        for act in pend:
            act()

    def start(src, dst, ssem, rsem, ctx, head):
        pltpu.make_async_remote_copy(
            src_ref=src, dst_ref=dst, send_sem=ssem, recv_sem=rsem,
            device_id=(ctx, head), device_id_type=MESH,
        ).start()

    def drain(ref, sem):
        pltpu.make_async_copy(ref, ref, sem).wait()

    def send_group(src_of, dst, index):
        each_group(lambda t, xp, hp: start(
            src_of(t, xp, hp), dst.at[me], s_one.at[index], r_one.at[index], z * XN + xp, hp))
        pend.append(lambda: drain(dst.at[pl.ds(0, GN - 1)], s_one.at[index]))

    def recv_group(dst, index):
        drain(dst.at[pl.ds(0, GN - 1)], r_one.at[index])

    def send_x(src_of, dst, index):
        def step(i, carry):
            xp = (x + swing(i, XN)) % XN
            start(src_of(xp), dst.at[x], s_one.at[index], r_one.at[index], z * XN + xp, h)
            return carry
        lax.fori_loop(0, XN - 1, step, 0)
        pend.append(lambda: drain(dst.at[pl.ds(0, XN - 1)], s_one.at[index]))

    def recv_x(dst, index):
        drain(dst.at[pl.ds(0, XN - 1)], r_one.at[index])

    def send_z(src_of, dst, index, low, high):
        def act(zp):
            @pl.when((zp >= low) & (zp < high))
            def _():
                start(src_of(zp), dst.at[z], s_two.at[index, zp], r_two.at[index, z], zp * XN + x, h)
        each_z(act)
        pend.append(lambda: wait_z(dst, s_two, index, low, high))

    def wait_z(dst, sems, index, low, high):
        def step(zp, carry):
            @pl.when(zp != z)
            def _():
                drain(dst.at[zp], sems.at[index, zp])
            return carry
        lax.fori_loop(low, high, step, 0)

    loads[0].wait()
    loads[1].wait()
    upper, lower = features(k_ref[...], kw_ref[...])
    kf[:, :D] = upper
    kf[:, D:] = lower
    kh[...], kl[...] = split(kf[...])
    loads[2].wait()
    vh[:, :D], vl[:, :D] = split(v_ref[...])
    vh[:, D:] = jnp.ones((ROWS, D), BF16)
    vl[:, D:] = jnp.zeros((ROWS, D), BF16)
    tot = []
    for c in range(NC):
        r = pl.ds(c * CH, CH)
        st[c] = mm3((kh[r, :], kl[r, :]), (vh[r, :D], vl[r, :D]), TN)
        tot.append((jnp.sum(kf[r, :D], axis=0, keepdims=True), jnp.sum(kf[r, D:], axis=0, keepdims=True)))
    tot_all = jnp.concatenate([tot[0][0] + tot[1][0], tot[0][1] + tot[1][1]], axis=0)
    mine = st[0, pl.ds(h * (XN * TR), XN * TR), :] + st[1, pl.ds(h * (XN * TR), XN * TR), :]
    for i in range(XN):
        sa[i, :TR] = mine[TR * i:TR * i + TR]
        sa[i, TR:TM] = tot_all
    pl.semaphore_wait(barrier, GN - 1 + ZN - 1)
    send_x(lambda xp: sa.at[xp, pl.ds(0, TM)], ra.at[:, pl.ds(0, TM)], 0)
    ra[x] = sa[x]

    for load in loads[3:]:
        load.wait()
    kth[...], ktl[...] = split(jnp.transpose(k_ref[...]))

    ids = ids_ref[...]
    onehot = (lax.broadcasted_iota(jnp.int32, (64, ROWS), 0) == ids).astype(F32).astype(BF16)
    diag = lax.broadcasted_iota(jnp.int32, (64, 64), 0) == lax.broadcasted_iota(jnp.int32, (64, 64), 1)
    wcol = jnp.sum(jnp.where(diag, sw_ref[...], 0.0), axis=1, keepdims=True)
    wtab = jnp.broadcast_to(wcol, (64, D))
    w1, rest = wtab.astype(BF16), wtab - wtab.astype(BF16).astype(F32)
    w2, w3 = split(rest)
    weight = dot(onehot, w1, TN) + dot(onehot, w2, TN) + dot(onehot, w3, TN)
    mask = lax.broadcasted_iota(jnp.int32, (CH, CH), 0) >= lax.broadcasted_iota(jnp.int32, (CH, CH), 1)

    def before(n):
        lanes = pl.ds(n * D, D)
        scaled[n] = c_ref[:, lanes] * weight
        upper, lower = features(q_ref[:, lanes], qw_ref[n])
        qf[n, :, :D] = upper
        qf[n, :, D:] = lower
        qh[n], ql[n] = split(qf[n])
        qth[n], qtl[n] = split(jnp.transpose(qf[n]))
        for c in range(NC):
            r = pl.ds(c * CH, CH)
            s = mm3((qh[n, r, :], ql[n, r, :]), (kh[r, :], kl[r, :]), NT)
            sh[n, r, :], sl[n, r, :] = split(jnp.where(mask, s, 0.0))
            intra[n, r, :] = mm3((sh[n, r, :], sl[n, r, :]), (vh[r, :], vl[r, :]), NN)

    recv_x(ra.at[:, pl.ds(0, TM)], 0)
    ta[...] = total(ra)
    send_z(lambda zp: ta.at[pl.ds(0, TM)], za.at[:, pl.ds(0, TM)], 0, z + 1, ZN)
    before(0)
    wait_z(za.at[:, pl.ds(0, TM)], r_two, 0, 0, z)
    pre = jnp.sum(za[...], axis=0)
    pre_tot = pre[TR:TM]
    for i in range(XN):
        gas[i] = pre[:TR]
        if i < XN - 1:
            pre = pre + ra[i]
            pre_tot = pre_tot + jnp.where(i < x, ra[i, TR:TM], 0.0)
    send_group(lambda t, xp, hp: gas.at[xp], ga, 1)
    ga[me] = gas[x]
    before(1)
    recv_group(ga, 1)

    p_now = ga[...].reshape(2 * D, D)
    tot_now = (pre_tot[0:1], pre_tot[1:2])
    states, totals = [], []
    for c in range(NC):
        states.append(split(p_now))
        totals.append(tot_now)
        if c < NC - 1:
            p_now = p_now + st[c]
            tot_now = (tot_now[0] + tot[c][0], tot_now[1] + tot[c][1])
    ct = [[0.0, 0.0] for _ in range(NC)]
    carried = []
    for c in range(NC):
        r = pl.ds(c * CH, CH)
        thi, tlo = split(jnp.concatenate([column(totals[c][0]), column(totals[c][1])], axis=0))
        full = (jnp.concatenate([states[c][0], thi], axis=1), jnp.concatenate([states[c][1], tlo], axis=1))
        acc = None
        for n in range(2):
            q = (qh[n, r, :], ql[n, r, :])
            nn = intra[n, r, :] + mm3(q, full, NN)
            inv = 1.0 / nn[:, D:]
            sc = scaled[n, r, :]
            gnum = sc * inv
            gno = -jnp.sum(sc * (nn[:, :D] * inv), axis=1, keepdims=True) * inv
            gnorm[n, r, :] = gno
            g = split(gnum)
            gnh[n, r, :], gnl[n, r, :] = g
            ct[c][0] = ct[c][0] + jnp.sum(gno * qf[n, r, :D], axis=0, keepdims=True)
            ct[c][1] = ct[c][1] + jnp.sum(gno * qf[n, r, D:], axis=0, keepdims=True)
            term = mm3((qth[n, :, r], qtl[n, :, r]), g, NN)
            acc = term if acc is None else acc + term
        carried.append(acc)
    c1[...] = carried[1]
    whole = carried[0] + carried[1]
    ct_all = jnp.concatenate([ct[0][0] + ct[1][0], ct[0][1] + ct[1][1]], axis=0)
    for t in range(GN):
        cb[t, :TR] = whole[TR * t:TR * t + TR]
        cb[t, TR:TM] = ct_all
    send_group(lambda t, xp, hp: cb.at[t, pl.ds(0, TM)], rb.at[:, pl.ds(0, TM)], 2)
    rb[me] = cb[me]

    def after(n):
        lanes = pl.ds(n * D, D)
        wpair = split(qw_ref[n])
        xs = split(q_ref[:, lanes])
        grads = []
        for c in range(NC):
            r = pl.ds(c * CH, CH)
            g = (gnh[n, r, :], gnl[n, r, :])
            gno = gnorm[n, r, :]
            gs = mm3(g, (vh[r, :D], vl[r, :D]), NT) + jnp.concatenate([gno, gno], axis=1)
            gs = split(jnp.where(mask, gs, 0.0))
            gfeat = mm3(gs, (kh[r, :], kl[r, :]), NN) + mm3(g, states[c], NT)
            a = gfeat[:, :D] + gno * totals[c][0]
            b = gfeat[:, D:] + gno * totals[c][1]
            gl = split(back(qf[n, r, :D], qf[n, r, D:], a, b))
            grads.append(gl)
            gq_ref[r, lanes] = mm3(gl, wpair, NT)
            gk = mm3(gs, (qh[n, r, :], ql[n, r, :]), TN)
            gv = mm3((sh[n, r, :], sl[n, r, :]), g, TN)
            if n == 0:
                gkf[r, :] = gk
                gval[r, :] = gv
            else:
                gkf[r, :] += gk
                gval[r, :] += gv
        gl = (jnp.concatenate([g[0] for g in grads], axis=0), jnp.concatenate([g[1] for g in grads], axis=0))
        gw = mm3(xs, gl, TN)
        parts = XN // 2
        for i in range(parts):
            qs[parts * n + i] = gw[QX * i:QX * i + QX]

    after(0)
    recv_group(rb.at[:, pl.ds(0, TM)], 2)
    by_x = []
    for i in range(XN):
        s = rb[i]
        for hp in range(1, HN):
            s = s + rb[hp * XN + i]
        by_x.append(s)
    tb[...] = total(by_x)
    send_z(lambda zp: tb.at[pl.ds(0, TM)], zb.at[:, pl.ds(0, TM)], 1, 0, z)
    after(1)
    stores[0].start()
    send_x(lambda xp: qs.at[xp], rq, 3)
    rq[x] = qs[x]

    r = pl.ds(0, CH)
    cpair = split(c1[...])
    gkf[r, :] += mm3((vh[r, :D], vl[r, :D]), cpair, NT) + jnp.concatenate([ct[1][0], ct[1][1]], axis=1)
    gval[r, :] += mm3((kh[r, :], kl[r, :]), cpair, NN)
    gl = back(kf[:, :D], kf[:, D:], gkf[:, :D], gkf[:, D:])
    for i in range(HN):
        ks[i, :, :D] = gl[OWN * i:OWN * i + OWN]
        ks[i, :, D:] = gval[OWN * i:OWN * i + OWN, :]

    kpair = (kth[...], ktl[...])
    gkw = mm3(kpair, split(gl), NN)
    for i in range(GN):
        iks[i] = gkw[KW * i:KW * i + KW]
    send_group(lambda t, xp, hp: iks.at[t], ikr, 9)
    ikr[me] = iks[me]

    wait_z(zb.at[:, pl.ds(0, TM)], r_two, 1, z + 1, ZN)
    suf = jnp.sum(zb[...], axis=0)
    suf_tot = suf[TR:TM]
    for i in reversed(range(XN)):
        gbs[i] = suf[:TR]
        if i > 0:
            suf = suf + by_x[i]
            suf_tot = suf_tot + jnp.where(i > x, by_x[i][TR:TM], 0.0)
    send_group(lambda t, xp, hp: gbs.at[xp], gb, 4)
    gb[me] = gbs[x]

    recv_x(rq, 3)
    tsum = total(rq)
    for i in range(ZN):
        tq[i] = tsum[QZ * i:QZ * i + QZ]
    send_z(lambda zp: tq.at[zp], zq, 2, 0, ZN)
    zq[z] = tq[z]
    recv_group(ikr, 9)
    early = jnp.sum(ikr[...], axis=0)

    recv_group(gb, 4)
    later = split(gb[...].reshape(2 * D, D))
    gfeat = mm3((vh[:, :D], vl[:, :D]), later, NT)
    gl = back(kf[:, :D], kf[:, D:], gfeat[:, :D] + suf_tot[0:1], gfeat[:, D:] + suf_tot[1:2])
    gkw = mm3(kpair, split(gl), NN)
    for i in range(GN):
        ck[i] = gkw[KW * i:KW * i + KW]
    send_x(lambda xp: ck.at[h * XN + xp], rc, 6)
    rc[x] = ck[me]
    gint[...] = gl

    def send_key(i, carry):
        hp = (h + i) % HN
        start(ks.at[hp], kr.at[h], s_one.at[5], r_one.at[5], pos, hp)
        return carry
    lax.fori_loop(1, HN, send_key, 0)
    pend.append(lambda: drain(kr.at[pl.ds(0, HN - 1)], s_one.at[5]))
    kr[h] = ks[h]

    wait_z(zq, r_two, 2, 0, ZN)
    gzs[...] = jnp.sum(zq[...], axis=0)
    send_z(lambda zp: gzs, gz, 3, 0, ZN)
    gz[z] = gzs[...]

    recv_x(rc, 6)
    tc[...] = total(rc) + early
    send_z(lambda zp: tc, zc, 4, 0, ZN)
    zc[z] = tc[...]

    wait_z(gz, r_two, 3, 0, ZN)
    send_x(lambda xp: gz, gx, 7)
    gx[x] = gz[...]

    wait_z(zc, r_two, 4, 0, ZN)
    gcs[...] = jnp.sum(zc[...], axis=0)
    send_group(lambda t, xp, hp: gcs, gc, 8)
    gc[me] = gcs[...]
    last = pend.pop()

    recv_x(gx, 7)
    for i in range(XN):
        for j in range(ZN):
            row = QX * i + QZ * j
            gqw_ref[row // D, row % D:row % D + QZ, :] = gx[i, j]
    stores[3].start()
    own = pl.ds(h * OWN, OWN)
    drain(kr.at[pl.ds(0, HN - 1)], r_one.at[5])
    got = kr[0]
    for i in range(1, HN):
        got = got + kr[i]
    gk_ref[...] = mm3(split(gint[own, :] + got[:, :D]), split(kw_ref[...]), NT)
    gv_ref[...] = mm3((kh[own, :], kl[own, :]), later, NN) + got[:, D:]
    stores[1].start()
    stores[2].start()
    finish()
    recv_group(gc, 8)
    for i in range(GN):
        gkw_ref[KW * i:KW * i + KW, :] = gc[i]
    stores[4].start()
    last()
    for copy in stores:
        copy.wait()


def store(*refs):
    sources, targets, held, sems = refs[:5], refs[5:10], refs[10:15], refs[15]
    reads = [pltpu.make_async_copy(sources[i], held[i], sems.at[0, i]) for i in range(5)]
    writes = [pltpu.make_async_copy(held[i], targets[i], sems.at[1, i]) for i in range(5)]
    for read in reads:
        read.start()
    for read, write in zip(reads, writes):
        read.wait()
        write.start()
    for write in writes:
        write.wait()


def on_device(queries, keys, values, cotangent, source_ids, source_weights, q_feature, k_feature):
    def vm(*shape, dtype=F32):
        return pltpu.VMEM(shape, dtype)

    b = dict(dtype=BF16)
    results = pl.pallas_call(
        kernel,
        out_shape=(
            jax.ShapeDtypeStruct((ROWS, 2 * D), F32),
            jax.ShapeDtypeStruct((OWN, D), F32),
            jax.ShapeDtypeStruct((OWN, D), F32),
            jax.ShapeDtypeStruct((2, D, D), F32),
            jax.ShapeDtypeStruct((D, D), F32),
        ),
        in_specs=[pl.BlockSpec(memory_space=pl.ANY)] * 8,
        out_specs=[pl.BlockSpec(memory_space=pl.ANY)] * 5,
        scratch_shapes=[
            vm(ROWS, 2 * D), vm(OWN, D), vm(OWN, D), vm(2, D, D), vm(D, D), pltpu.SemaphoreType.DMA((5,)),
            vm(ROWS, 2 * D), vm(ROWS, D), vm(ROWS, D), vm(ROWS, 2 * D), vm(1, ROWS, dtype=jnp.int32), vm(1, 64),
            vm(2, D, D), vm(D, D), pltpu.SemaphoreType.DMA((8,)),
            vm(ROWS, 2 * D), vm(ROWS, 2 * D, **b), vm(ROWS, 2 * D, **b),
            vm(ROWS, 2 * D, **b), vm(ROWS, 2 * D, **b),
            vm(2, ROWS, 2 * D), vm(2, ROWS, 2 * D, **b), vm(2, ROWS, 2 * D, **b),
            vm(2, ROWS, CH, **b), vm(2, ROWS, CH, **b),
            vm(2, ROWS, 2 * D), vm(2, ROWS, D), vm(NC, 2 * D, D),
            vm(2, ROWS, D, **b), vm(2, ROWS, D, **b), vm(2, ROWS, D),
            vm(2 * D, D), vm(ROWS, 2 * D), vm(ROWS, D),
            vm(XN, TP, D), vm(XN, TP, D), vm(TP, D), vm(ZN, TP, D), vm(XN, TR, D), vm(GN, TR, D),
            vm(GN, TP, D), vm(GN, TP, D), vm(TP, D), vm(ZN, TP, D), vm(XN, TR, D), vm(GN, TR, D),
            vm(HN, OWN, 2 * D), vm(HN, OWN, 2 * D),
            vm(XN, QX, D), vm(XN, QX, D), vm(ZN, QZ, D), vm(ZN, QZ, D),
            vm(QZ, D), vm(ZN, QZ, D), vm(XN, ZN, QZ, D),
            vm(GN, KW, D), vm(XN, KW, D), vm(KW, D), vm(ZN, KW, D), vm(KW, D), vm(GN, KW, D),
            vm(2, 2 * D, ROWS, **b), vm(2, 2 * D, ROWS, **b), vm(D, ROWS, **b), vm(D, ROWS, **b),
            vm(GN, KW, D), vm(GN, KW, D), vm(ROWS, D),
            pltpu.SemaphoreType.DMA((10,)),
            pltpu.SemaphoreType.DMA((5, ZN)),
            pltpu.SemaphoreType.DMA((10,)),
            pltpu.SemaphoreType.DMA((5, ZN)),
        ],
        compiler_params=pltpu.CompilerParams(
            collective_id=0, has_side_effects=True, vmem_limit_bytes=60 * 1024 * 1024
        ),
        cost_estimate=pl.CostEstimate(flops=3_000_000_000, bytes_accessed=2_500_000, transcendentals=400_000),
    )(queries, keys, values, cotangent, source_ids.reshape(1, ROWS), source_weights.reshape(1, -1), q_feature, k_feature)
    return pl.pallas_call(
        store,
        out_shape=[jax.ShapeDtypeStruct(a.shape, a.dtype) for a in results],
        in_specs=[pl.BlockSpec(memory_space=pl.ANY)] * 5,
        out_specs=[pl.BlockSpec(memory_space=pl.ANY)] * 5,
        scratch_shapes=[pltpu.VMEM(a.shape, a.dtype) for a in results] + [pltpu.SemaphoreType.DMA((2, 5))],
        compiler_params=pltpu.CompilerParams(vmem_limit_bytes=60 * 1024 * 1024),
    )(*results)


def solution(mesh):
    placed = (
        P("ctx", "head"),
        P("ctx", None),
        P("ctx", None),
        P("ctx", "head"),
        P("ctx"),
        P(),
        P("head", None, None),
        P(),
    )
    return jax.shard_map(
        on_device,
        mesh=mesh,
        in_specs=placed,
        out_specs=(
            P("ctx", "head"),
            P(("ctx", "head"), None),
            P(("ctx", "head"), None),
            P("head", None, None),
            P(),
        ),
        check_vma=False,
    )
```

```python
import jax
import jax.numpy as jnp
from jax import lax
from jax.experimental import pallas as pl
from jax.experimental.pallas import tpu as pltpu
from jax.sharding import PartitionSpec as P

MESH = pl.DeviceIdType.MESH
F32 = jnp.float32
BF16 = jnp.bfloat16
NN = ((1,), (0,))
NT = ((1,), (1,))
TN = ((0,), (0,))
XN = 4
ZN = 16
HN = 8
GN = XN * HN
ROWS = 512
CH = 256
D = 128
NC = ROWS // CH
OWN = ROWS // HN
TR = 2 * D // GN
TM = TR + 2
TP = TR + 8
KW = D // GN
QX = 2 * D // XN
QZ = QX // ZN


def split(a):
    high = a.astype(BF16)
    return high, (a - high.astype(F32)).astype(BF16)


def dot(a, b, dims):
    return lax.dot_general(a, b, (dims, ((), ())), preferred_element_type=F32)


def mm3(a, b, dims):
    (ah, al), (bh, bl) = a, b
    return dot(ah, bh, dims) + (dot(ah, bl, dims) + dot(al, bh, dims))


def total(parts):
    acc = parts[0]
    for i in range(1, XN):
        acc = acc + parts[i]
    return acc


def features(inputs, weight):
    logits = jnp.dot(inputs, weight, precision=lax.Precision.HIGHEST, preferred_element_type=F32)
    upper = jnp.exp(logits - jnp.max(logits, axis=1, keepdims=True))
    lower = jnp.exp(jnp.min(logits, axis=1, keepdims=True) - logits)
    upper = upper * (1.0 / jnp.sum(upper, axis=1, keepdims=True))
    lower = lower * (1.0 / jnp.sum(lower, axis=1, keepdims=True))
    return upper, lower


def back(upper, lower, a, b):
    up = upper * (a - jnp.sum(upper * a, axis=1, keepdims=True))
    return up - lower * (b - jnp.sum(lower * b, axis=1, keepdims=True))


def column(row):
    return jnp.transpose(jnp.broadcast_to(row, (D, D)))


def swing(i, n):
    return (n // 2 + ((i + 1) // 2) * (1 - 2 * (i % 2))) % n


def kernel(
    q_in, k_in, v_in, c_in, ids_in, sw_in, qw_in, kw_in,
    gq_out, gk_out, gv_out, gqw_out, gkw_out,
    gq_ref, gk_ref, gv_ref, gqw_ref, gkw_ref, o_sem,
    q_ref, k_ref, v_ref, c_ref, ids_ref, sw_ref, qw_ref, kw_ref, i_sem,
    kf, kh, kl, vh, vl, qf, qh, ql, sh, sl, intra, scaled, st, gnh, gnl, gnorm, c1, gkf, gval,
    sa, ra, ta, za, gas, ga, cb, rb, tb, zb, gbs, gb, ks, kr, qs, rq, tq, zq, gzs, gz, gx, ck, rc, tc, zc, gcs, gc,
    qth, qtl, kth, ktl, iks, ikr, gint,
    s_one, s_two, r_one, r_two, ready,
):
    pos = lax.axis_index("ctx")
    h = lax.axis_index("head")
    z = pos // XN
    x = pos % XN
    me = h * XN + x

    def each_group(act):
        def step(i, carry):
            xp = (x + swing(i // HN, XN)) % XN
            yp = (h // 2 + swing(i // 2 % (HN // 2), HN // 2)) % (HN // 2)
            hp = yp * 2 + (h + i + 1) % 2
            act(hp * XN + xp, xp, hp)
            return carry
        lax.fori_loop(0, GN - 1, step, 0)

    def each_z(act):
        def step(i, carry):
            act((z + swing(i, ZN)) % ZN)
            return carry
        lax.fori_loop(0, ZN - 1, step, 0)

    barrier = pltpu.get_barrier_semaphore()

    def greet(ctx, head):
        pl.semaphore_signal(barrier, inc=1, device_id=(ctx, head), device_id_type=MESH)

    loads = [
        pltpu.make_async_copy(src, dst, i_sem.at[i])
        for i, (src, dst) in enumerate([
            (k_in, k_ref), (kw_in, kw_ref), (v_in, v_ref), (q_in, q_ref),
            (qw_in, qw_ref), (c_in, c_ref), (ids_in, ids_ref), (sw_in, sw_ref),
        ])
    ]
    for load in loads:
        load.start()
    stores = [
        pltpu.make_async_copy(src, dst, o_sem.at[i])
        for i, (src, dst) in enumerate([
            (gq_ref, gq_out), (gk_ref, gk_out), (gv_ref, gv_out), (gqw_ref, gqw_out), (gkw_ref, gkw_out),
        ])
    ]
    za[...] = jnp.zeros_like(za)
    zb[...] = jnp.zeros_like(zb)
    core = h % 2
    first = h - core

    def greet_x(i, carry):
        greet(z * XN + (x + swing(i, XN)) % XN, first)
        return carry
    lax.fori_loop(0, XN - 1, greet_x, 0)

    @pl.when(core == 1)
    def _():
        greet(pos, first)
    each_z(lambda zp: greet(zp * XN + x, first + 1))

    def greet_chip(i, carry):
        yp = (h // 2 + swing(i % (HN // 2), HN // 2)) % (HN // 2)
        greet(z * XN + (x + swing(i // (HN // 2), XN)) % XN, yp * 2 + 1)
        return carry
    lax.fori_loop(0, GN // 2 - 1, greet_chip, 0)

    @pl.when(core == 0)
    def _():
        greet(pos, first + 1)

    pend = []

    def finish():
        for act in pend:
            act()

    def start(src, dst, ssem, rsem, ctx, head):
        pltpu.make_async_remote_copy(
            src_ref=src, dst_ref=dst, send_sem=ssem, recv_sem=rsem,
            device_id=(ctx, head), device_id_type=MESH,
        ).start()

    def drain(ref, sem):
        pltpu.make_async_copy(ref, ref, sem).wait()

    def send_group(src_of, dst, index):
        each_group(lambda t, xp, hp: start(
            src_of(t, xp, hp), dst.at[me], s_one.at[index], r_one.at[index], z * XN + xp, hp))
        pend.append(lambda: drain(dst.at[pl.ds(0, GN - 1)], s_one.at[index]))

    def recv_group(dst, index):
        drain(dst.at[pl.ds(0, GN - 1)], r_one.at[index])

    def send_x(src_of, dst, index):
        def step(i, carry):
            xp = (x + swing(i, XN)) % XN
            start(src_of(xp), dst.at[x], s_one.at[index], r_one.at[index], z * XN + xp, h)
            return carry
        lax.fori_loop(0, XN - 1, step, 0)
        pend.append(lambda: drain(dst.at[pl.ds(0, XN - 1)], s_one.at[index]))

    def recv_x(dst, index):
        drain(dst.at[pl.ds(0, XN - 1)], r_one.at[index])

    def send_z(src_of, dst, index, low, high):
        def act(zp):
            @pl.when((zp >= low) & (zp < high))
            def _():
                start(src_of(zp), dst.at[z], s_two.at[index, zp], r_two.at[index, z], zp * XN + x, h)
        each_z(act)
        pend.append(lambda: wait_z(dst, s_two, index, low, high))

    def wait_z(dst, sems, index, low, high):
        def step(zp, carry):
            @pl.when(zp != z)
            def _():
                drain(dst.at[zp], sems.at[index, zp])
            return carry
        lax.fori_loop(low, high, step, 0)

    loads[0].wait()
    loads[1].wait()
    upper, lower = features(k_ref[...], kw_ref[...])
    kf[:, :D] = upper
    kf[:, D:] = lower
    kh[...], kl[...] = split(kf[...])
    loads[2].wait()
    vh[:, :D], vl[:, :D] = split(v_ref[...])
    vh[:, D:] = jnp.ones((ROWS, D), BF16)
    vl[:, D:] = jnp.zeros((ROWS, D), BF16)
    tot = []
    for c in range(NC):
        r = pl.ds(c * CH, CH)
        st[c] = mm3((kh[r, :], kl[r, :]), (vh[r, :D], vl[r, :D]), TN)
        tot.append((jnp.sum(kf[r, :D], axis=0, keepdims=True), jnp.sum(kf[r, D:], axis=0, keepdims=True)))
    tot_all = jnp.concatenate([tot[0][0] + tot[1][0], tot[0][1] + tot[1][1]], axis=0)
    mine = st[0, pl.ds(h * (XN * TR), XN * TR), :] + st[1, pl.ds(h * (XN * TR), XN * TR), :]
    for i in range(XN):
        sa[i, :TR] = mine[TR * i:TR * i + TR]
        sa[i, TR:TM] = tot_all
    @pl.when(core == 0)
    def _():
        pl.semaphore_wait(barrier, 2 * (XN - 1) + 1)
        pl.semaphore_signal(ready.at[0], inc=1, device_id=(pos, first + 1), device_id_type=MESH)

    @pl.when(core == 1)
    def _():
        pl.semaphore_wait(ready.at[0], 1)
    send_x(lambda xp: sa.at[xp, pl.ds(0, TM)], ra.at[:, pl.ds(0, TM)], 0)
    ra[x] = sa[x]

    for load in loads[3:]:
        load.wait()
    kth[...], ktl[...] = split(jnp.transpose(k_ref[...]))

    ids = ids_ref[...]
    onehot = (lax.broadcasted_iota(jnp.int32, (64, ROWS), 0) == ids).astype(F32).astype(BF16)
    diag = lax.broadcasted_iota(jnp.int32, (64, 64), 0) == lax.broadcasted_iota(jnp.int32, (64, 64), 1)
    wcol = jnp.sum(jnp.where(diag, sw_ref[...], 0.0), axis=1, keepdims=True)
    wtab = jnp.broadcast_to(wcol, (64, D))
    w1, rest = wtab.astype(BF16), wtab - wtab.astype(BF16).astype(F32)
    w2, w3 = split(rest)
    weight = dot(onehot, w1, TN) + dot(onehot, w2, TN) + dot(onehot, w3, TN)
    mask = lax.broadcasted_iota(jnp.int32, (CH, CH), 0) >= lax.broadcasted_iota(jnp.int32, (CH, CH), 1)

    def before(n):
        lanes = pl.ds(n * D, D)
        scaled[n] = c_ref[:, lanes] * weight
        upper, lower = features(q_ref[:, lanes], qw_ref[n])
        qf[n, :, :D] = upper
        qf[n, :, D:] = lower
        qh[n], ql[n] = split(qf[n])
        qth[n], qtl[n] = split(jnp.transpose(qf[n]))
        for c in range(NC):
            r = pl.ds(c * CH, CH)
            s = mm3((qh[n, r, :], ql[n, r, :]), (kh[r, :], kl[r, :]), NT)
            sh[n, r, :], sl[n, r, :] = split(jnp.where(mask, s, 0.0))
            intra[n, r, :] = mm3((sh[n, r, :], sl[n, r, :]), (vh[r, :], vl[r, :]), NN)

    @pl.when(core == 1)
    def _():
        pl.semaphore_wait(barrier, 2 * (ZN - 1) + GN - 1)
        pl.semaphore_signal(ready.at[1], inc=1, device_id=(pos, first), device_id_type=MESH)

    @pl.when(core == 0)
    def _():
        pl.semaphore_wait(ready.at[1], 1)
    recv_x(ra.at[:, pl.ds(0, TM)], 0)
    ta[...] = total(ra)
    send_z(lambda zp: ta.at[pl.ds(0, TM)], za.at[:, pl.ds(0, TM)], 0, z + 1, ZN)
    before(0)
    wait_z(za.at[:, pl.ds(0, TM)], r_two, 0, 0, z)
    pre = jnp.sum(za[...], axis=0)
    pre_tot = pre[TR:TM]
    for i in range(XN):
        gas[i] = pre[:TR]
        if i < XN - 1:
            pre = pre + ra[i]
            pre_tot = pre_tot + jnp.where(i < x, ra[i, TR:TM], 0.0)
    send_group(lambda t, xp, hp: gas.at[xp], ga, 1)
    ga[me] = gas[x]
    before(1)
    recv_group(ga, 1)

    p_now = ga[...].reshape(2 * D, D)
    tot_now = (pre_tot[0:1], pre_tot[1:2])
    states, totals = [], []
    for c in range(NC):
        states.append(split(p_now))
        totals.append(tot_now)
        if c < NC - 1:
            p_now = p_now + st[c]
            tot_now = (tot_now[0] + tot[c][0], tot_now[1] + tot[c][1])
    ct = [[0.0, 0.0] for _ in range(NC)]
    carried = []
    for c in range(NC):
        r = pl.ds(c * CH, CH)
        thi, tlo = split(jnp.concatenate([column(totals[c][0]), column(totals[c][1])], axis=0))
        full = (jnp.concatenate([states[c][0], thi], axis=1), jnp.concatenate([states[c][1], tlo], axis=1))
        acc = None
        for n in range(2):
            q = (qh[n, r, :], ql[n, r, :])
            nn = intra[n, r, :] + mm3(q, full, NN)
            inv = 1.0 / nn[:, D:]
            sc = scaled[n, r, :]
            gnum = sc * inv
            gno = -jnp.sum(sc * (nn[:, :D] * inv), axis=1, keepdims=True) * inv
            gnorm[n, r, :] = gno
            g = split(gnum)
            gnh[n, r, :], gnl[n, r, :] = g
            ct[c][0] = ct[c][0] + jnp.sum(gno * qf[n, r, :D], axis=0, keepdims=True)
            ct[c][1] = ct[c][1] + jnp.sum(gno * qf[n, r, D:], axis=0, keepdims=True)
            term = mm3((qth[n, :, r], qtl[n, :, r]), g, NN)
            acc = term if acc is None else acc + term
        carried.append(acc)
    c1[...] = carried[1]
    whole = carried[0] + carried[1]
    ct_all = jnp.concatenate([ct[0][0] + ct[1][0], ct[0][1] + ct[1][1]], axis=0)
    for t in range(GN):
        cb[t, :TR] = whole[TR * t:TR * t + TR]
        cb[t, TR:TM] = ct_all
    send_group(lambda t, xp, hp: cb.at[t, pl.ds(0, TM)], rb.at[:, pl.ds(0, TM)], 2)
    rb[me] = cb[me]

    grads = [[], []]

    def after(n, parts):
        lanes = pl.ds(n * D, D)
        wpair = split(qw_ref[n])
        for c in parts:
            r = pl.ds(c * CH, CH)
            g = (gnh[n, r, :], gnl[n, r, :])
            gno = gnorm[n, r, :]
            gs = mm3(g, (vh[r, :D], vl[r, :D]), NT) + jnp.concatenate([gno, gno], axis=1)
            gs = split(jnp.where(mask, gs, 0.0))
            gfeat = mm3(gs, (kh[r, :], kl[r, :]), NN) + mm3(g, states[c], NT)
            a = gfeat[:, :D] + gno * totals[c][0]
            b = gfeat[:, D:] + gno * totals[c][1]
            gl = split(back(qf[n, r, :D], qf[n, r, D:], a, b))
            grads[n].append(gl)
            gq_ref[r, lanes] = mm3(gl, wpair, NT)
            gk = mm3(gs, (qh[n, r, :], ql[n, r, :]), TN)
            gv = mm3((sh[n, r, :], sl[n, r, :]), g, TN)
            if n == 0:
                gkf[r, :] = gk
                gval[r, :] = gv
            else:
                gkf[r, :] += gk
                gval[r, :] += gv

    def weight_grad(n):
        gl = tuple(jnp.concatenate([g[i] for g in grads[n]], axis=0) for i in range(2))
        gw = mm3(split(q_ref[:, n * D:n * D + D]), gl, TN)
        parts = XN // 2
        for i in range(parts):
            qs[parts * n + i] = gw[QX * i:QX * i + QX]

    after(0, (0, 1))
    weight_grad(0)
    after(1, (0,))
    recv_group(rb.at[:, pl.ds(0, TM)], 2)
    by_x = []
    for i in range(XN):
        s = rb[i]
        for hp in range(1, HN):
            s = s + rb[hp * XN + i]
        by_x.append(s)
    tb[...] = total(by_x)
    send_z(lambda zp: tb.at[pl.ds(0, TM)], zb.at[:, pl.ds(0, TM)], 1, 0, z)
    after(1, (1,))
    weight_grad(1)
    stores[0].start()
    send_x(lambda xp: qs.at[xp], rq, 3)
    rq[x] = qs[x]

    r = pl.ds(0, CH)
    cpair = split(c1[...])
    gkf[r, :] += mm3((vh[r, :D], vl[r, :D]), cpair, NT) + jnp.concatenate([ct[1][0], ct[1][1]], axis=1)
    gval[r, :] += mm3((kh[r, :], kl[r, :]), cpair, NN)
    gl = back(kf[:, :D], kf[:, D:], gkf[:, :D], gkf[:, D:])
    for i in range(HN):
        ks[i, :, :D] = gl[OWN * i:OWN * i + OWN]
        ks[i, :, D:] = gval[OWN * i:OWN * i + OWN, :]

    kpair = (kth[...], ktl[...])
    gkw = mm3(kpair, split(gl), NN)
    for i in range(GN):
        iks[i] = gkw[KW * i:KW * i + KW]
    send_group(lambda t, xp, hp: iks.at[t], ikr, 9)
    ikr[me] = iks[me]

    wait_z(zb.at[:, pl.ds(0, TM)], r_two, 1, z + 1, ZN)
    suf = jnp.sum(zb[...], axis=0)
    suf_tot = suf[TR:TM]
    for i in reversed(range(XN)):
        gbs[i] = suf[:TR]
        if i > 0:
            suf = suf + by_x[i]
            suf_tot = suf_tot + jnp.where(i > x, by_x[i][TR:TM], 0.0)
    send_group(lambda t, xp, hp: gbs.at[xp], gb, 4)
    gb[me] = gbs[x]

    recv_x(rq, 3)
    tsum = total(rq)
    for i in range(ZN):
        tq[i] = tsum[QZ * i:QZ * i + QZ]
    send_z(lambda zp: tq.at[zp], zq, 2, 0, ZN)
    zq[z] = tq[z]
    recv_group(ikr, 9)
    early = jnp.sum(ikr[...], axis=0)

    recv_group(gb, 4)
    later = split(gb[...].reshape(2 * D, D))
    gfeat = mm3((vh[:, :D], vl[:, :D]), later, NT)
    gl = back(kf[:, :D], kf[:, D:], gfeat[:, :D] + suf_tot[0:1], gfeat[:, D:] + suf_tot[1:2])
    gkw = mm3(kpair, split(gl), NN)
    for i in range(GN):
        ck[i] = gkw[KW * i:KW * i + KW]
    send_x(lambda xp: ck.at[h * XN + xp], rc, 6)
    rc[x] = ck[me]
    gint[...] = gl

    def send_key(i, carry):
        hp = (h + i) % HN
        start(ks.at[hp], kr.at[h], s_one.at[5], r_one.at[5], pos, hp)
        return carry
    lax.fori_loop(1, HN, send_key, 0)
    pend.append(lambda: drain(kr.at[pl.ds(0, HN - 1)], s_one.at[5]))
    kr[h] = ks[h]

    wait_z(zq, r_two, 2, 0, ZN)
    gzs[...] = jnp.sum(zq[...], axis=0)
    send_z(lambda zp: gzs, gz, 3, 0, ZN)
    gz[z] = gzs[...]

    recv_x(rc, 6)
    tc[...] = total(rc) + early
    send_z(lambda zp: tc, zc, 4, 0, ZN)
    zc[z] = tc[...]

    wait_z(gz, r_two, 3, 0, ZN)
    send_x(lambda xp: gz, gx, 7)
    gx[x] = gz[...]

    wait_z(zc, r_two, 4, 0, ZN)
    gcs[...] = jnp.sum(zc[...], axis=0)
    send_group(lambda t, xp, hp: gcs, gc, 8)
    gc[me] = gcs[...]
    last = pend.pop()

    recv_x(gx, 7)
    for i in range(XN):
        for j in range(ZN):
            row = QX * i + QZ * j
            gqw_ref[row // D, row % D:row % D + QZ, :] = gx[i, j]
    stores[3].start()
    own = pl.ds(h * OWN, OWN)
    drain(kr.at[pl.ds(0, HN - 1)], r_one.at[5])
    got = kr[0]
    for i in range(1, HN):
        got = got + kr[i]
    gk_ref[...] = mm3(split(gint[own, :] + got[:, :D]), split(kw_ref[...]), NT)
    gv_ref[...] = mm3((kh[own, :], kl[own, :]), later, NN) + got[:, D:]
    stores[1].start()
    stores[2].start()
    finish()
    recv_group(gc, 8)
    for i in range(GN):
        gkw_ref[KW * i:KW * i + KW, :] = gc[i]
    stores[4].start()
    last()
    for copy in stores:
        copy.wait()


def store(*refs):
    sources, targets, held, sems = refs[:5], refs[5:10], refs[10:15], refs[15]
    reads = [pltpu.make_async_copy(sources[i], held[i], sems.at[0, i]) for i in range(5)]
    writes = [pltpu.make_async_copy(held[i], targets[i], sems.at[1, i]) for i in range(5)]
    for read in reads:
        read.start()
    for read, write in zip(reads, writes):
        read.wait()
        write.start()
    for write in writes:
        write.wait()


def on_device(queries, keys, values, cotangent, source_ids, source_weights, q_feature, k_feature):
    def vm(*shape, dtype=F32):
        return pltpu.VMEM(shape, dtype)

    b = dict(dtype=BF16)
    results = pl.pallas_call(
        kernel,
        out_shape=(
            jax.ShapeDtypeStruct((ROWS, 2 * D), F32),
            jax.ShapeDtypeStruct((OWN, D), F32),
            jax.ShapeDtypeStruct((OWN, D), F32),
            jax.ShapeDtypeStruct((2, D, D), F32),
            jax.ShapeDtypeStruct((D, D), F32),
        ),
        in_specs=[pl.BlockSpec(memory_space=pl.ANY)] * 8,
        out_specs=[pl.BlockSpec(memory_space=pl.ANY)] * 5,
        scratch_shapes=[
            vm(ROWS, 2 * D), vm(OWN, D), vm(OWN, D), vm(2, D, D), vm(D, D), pltpu.SemaphoreType.DMA((5,)),
            vm(ROWS, 2 * D), vm(ROWS, D), vm(ROWS, D), vm(ROWS, 2 * D), vm(1, ROWS, dtype=jnp.int32), vm(1, 64),
            vm(2, D, D), vm(D, D), pltpu.SemaphoreType.DMA((8,)),
            vm(ROWS, 2 * D), vm(ROWS, 2 * D, **b), vm(ROWS, 2 * D, **b),
            vm(ROWS, 2 * D, **b), vm(ROWS, 2 * D, **b),
            vm(2, ROWS, 2 * D), vm(2, ROWS, 2 * D, **b), vm(2, ROWS, 2 * D, **b),
            vm(2, ROWS, CH, **b), vm(2, ROWS, CH, **b),
            vm(2, ROWS, 2 * D), vm(2, ROWS, D), vm(NC, 2 * D, D),
            vm(2, ROWS, D, **b), vm(2, ROWS, D, **b), vm(2, ROWS, D),
            vm(2 * D, D), vm(ROWS, 2 * D), vm(ROWS, D),
            vm(XN, TP, D), vm(XN, TP, D), vm(TP, D), vm(ZN, TP, D), vm(XN, TR, D), vm(GN, TR, D),
            vm(GN, TP, D), vm(GN, TP, D), vm(TP, D), vm(ZN, TP, D), vm(XN, TR, D), vm(GN, TR, D),
            vm(HN, OWN, 2 * D), vm(HN, OWN, 2 * D),
            vm(XN, QX, D), vm(XN, QX, D), vm(ZN, QZ, D), vm(ZN, QZ, D),
            vm(QZ, D), vm(ZN, QZ, D), vm(XN, ZN, QZ, D),
            vm(GN, KW, D), vm(XN, KW, D), vm(KW, D), vm(ZN, KW, D), vm(KW, D), vm(GN, KW, D),
            vm(2, 2 * D, ROWS, **b), vm(2, 2 * D, ROWS, **b), vm(D, ROWS, **b), vm(D, ROWS, **b),
            vm(GN, KW, D), vm(GN, KW, D), vm(ROWS, D),
            pltpu.SemaphoreType.DMA((10,)),
            pltpu.SemaphoreType.DMA((5, ZN)),
            pltpu.SemaphoreType.DMA((10,)),
            pltpu.SemaphoreType.DMA((5, ZN)),
            pltpu.SemaphoreType.REGULAR((2,)),
        ],
        compiler_params=pltpu.CompilerParams(
            collective_id=0, has_side_effects=True, vmem_limit_bytes=60 * 1024 * 1024
        ),
        cost_estimate=pl.CostEstimate(flops=3_000_000_000, bytes_accessed=2_500_000, transcendentals=400_000),
    )(queries, keys, values, cotangent, source_ids.reshape(1, ROWS), source_weights.reshape(1, -1), q_feature, k_feature)
    return pl.pallas_call(
        store,
        out_shape=[jax.ShapeDtypeStruct(a.shape, a.dtype) for a in results],
        in_specs=[pl.BlockSpec(memory_space=pl.ANY)] * 5,
        out_specs=[pl.BlockSpec(memory_space=pl.ANY)] * 5,
        scratch_shapes=[pltpu.VMEM(a.shape, a.dtype) for a in results] + [pltpu.SemaphoreType.DMA((2, 5))],
        compiler_params=pltpu.CompilerParams(vmem_limit_bytes=60 * 1024 * 1024),
    )(*results)


def solution(mesh):
    placed = (
        P("ctx", "head"),
        P("ctx", None),
        P("ctx", None),
        P("ctx", "head"),
        P("ctx"),
        P(),
        P("head", None, None),
        P(),
    )
    return jax.shard_map(
        on_device,
        mesh=mesh,
        in_specs=placed,
        out_specs=(
            P("ctx", "head"),
            P(("ctx", "head"), None),
            P(("ctx", "head"), None),
            P("head", None, None),
            P(),
        ),
        check_vma=False,
    )
```

```python
import jax
import jax.numpy as jnp
from jax import lax
from jax.experimental import pallas as pl
from jax.experimental.pallas import tpu as pltpu
from jax.sharding import PartitionSpec as P

MESH = pl.DeviceIdType.MESH
F32 = jnp.float32
BF16 = jnp.bfloat16
NN = ((1,), (0,))
NT = ((1,), (1,))
TN = ((0,), (0,))
XN = 4
ZN = 16
HN = 8
GN = XN * HN
ROWS = 512
CH = 256
D = 128
NC = ROWS // CH
OWN = ROWS // HN
TR = 2 * D // GN
TM = TR + 2
TP = TR + 8
KW = D // GN
QX = 2 * D // XN
QZ = QX // ZN


def split(a):
    high = a.astype(BF16)
    return high, (a - high.astype(F32)).astype(BF16)


def dot(a, b, dims):
    return lax.dot_general(a, b, (dims, ((), ())), preferred_element_type=F32)


def mm3(a, b, dims):
    (ah, al), (bh, bl) = a, b
    return dot(ah, bh, dims) + (dot(ah, bl, dims) + dot(al, bh, dims))


def total(parts):
    acc = parts[0]
    for i in range(1, XN):
        acc = acc + parts[i]
    return acc


def features(inputs, weight):
    logits = jnp.dot(inputs, weight, precision=lax.Precision.HIGHEST, preferred_element_type=F32)
    upper = jnp.exp(logits - jnp.max(logits, axis=1, keepdims=True))
    lower = jnp.exp(jnp.min(logits, axis=1, keepdims=True) - logits)
    upper = upper * (1.0 / jnp.sum(upper, axis=1, keepdims=True))
    lower = lower * (1.0 / jnp.sum(lower, axis=1, keepdims=True))
    return upper, lower


def back(upper, lower, a, b):
    up = upper * (a - jnp.sum(upper * a, axis=1, keepdims=True))
    return up - lower * (b - jnp.sum(lower * b, axis=1, keepdims=True))


def column(row):
    return jnp.transpose(jnp.broadcast_to(row, (D, D)))


def swing(i, n):
    return (n // 2 + ((i + 1) // 2) * (1 - 2 * (i % 2))) % n


def kernel(
    q_in, k_in, v_in, c_in, ids_in, sw_in, qw_in, kw_in,
    gq_out, gk_out, gv_out, gqw_out, gkw_out,
    gq_ref, gk_ref, gv_ref, gqw_ref, gkw_ref, o_sem,
    q_ref, k_ref, v_ref, c_ref, ids_ref, sw_ref, qw_ref, kw_ref, i_sem,
    kf, kh, kl, vh, vl, qf, qh, ql, sh, sl, intra, scaled, st, gnh, gnl, gnorm, c1, gkf, gval,
    sa, ra, ta, za, gas, ga, cb, rb, tb, zb, gbs, gb, ks, kr, qs, rq, tq, zq, gzs, gz, gx, ck, rc, tc, zc, gcs, gc,
    qth, qtl, kth, ktl, iks, ikr, gint, invs, ctb, ctr, ctt, zct,
    s_one, s_two, r_one, r_two, ready,
):
    pos = lax.axis_index("ctx")
    h = lax.axis_index("head")
    z = pos // XN
    x = pos % XN
    me = h * XN + x

    def each_group(act):
        def step(i, carry):
            xp = (x + swing(i // HN, XN)) % XN
            yp = (h // 2 + swing(i // 2 % (HN // 2), HN // 2)) % (HN // 2)
            hp = yp * 2 + (h + i + 1) % 2
            act(hp * XN + xp, xp, hp)
            return carry
        lax.fori_loop(0, GN - 1, step, 0)

    def each_z(act):
        def step(i, carry):
            act((z + swing(i, ZN)) % ZN)
            return carry
        lax.fori_loop(0, ZN - 1, step, 0)

    barrier = pltpu.get_barrier_semaphore()

    def greet(ctx, head):
        pl.semaphore_signal(barrier, inc=1, device_id=(ctx, head), device_id_type=MESH)

    loads = [
        pltpu.make_async_copy(src, dst, i_sem.at[i])
        for i, (src, dst) in enumerate([
            (k_in, k_ref), (kw_in, kw_ref), (v_in, v_ref), (q_in, q_ref),
            (qw_in, qw_ref), (c_in, c_ref), (ids_in, ids_ref), (sw_in, sw_ref),
        ])
    ]
    for load in loads:
        load.start()
    stores = [
        pltpu.make_async_copy(src, dst, o_sem.at[i])
        for i, (src, dst) in enumerate([
            (gq_ref, gq_out), (gk_ref, gk_out), (gv_ref, gv_out), (gqw_ref, gqw_out), (gkw_ref, gkw_out),
        ])
    ]
    za[...] = jnp.zeros_like(za)
    zb[...] = jnp.zeros_like(zb)
    zct[...] = jnp.zeros_like(zct)
    core = h % 2
    first = h - core

    def greet_x(i, carry):
        greet(z * XN + (x + swing(i, XN)) % XN, first)
        return carry
    lax.fori_loop(0, XN - 1, greet_x, 0)

    @pl.when(core == 1)
    def _():
        greet(pos, first)
    each_z(lambda zp: greet(zp * XN + x, first + 1))

    def greet_chip(i, carry):
        yp = (h // 2 + swing(i % (HN // 2), HN // 2)) % (HN // 2)
        greet(z * XN + (x + swing(i // (HN // 2), XN)) % XN, yp * 2 + 1)
        return carry
    lax.fori_loop(0, GN // 2 - 1, greet_chip, 0)

    @pl.when(core == 0)
    def _():
        greet(pos, first + 1)

    pend = []

    def finish():
        for act in pend:
            act()

    def start(src, dst, ssem, rsem, ctx, head):
        pltpu.make_async_remote_copy(
            src_ref=src, dst_ref=dst, send_sem=ssem, recv_sem=rsem,
            device_id=(ctx, head), device_id_type=MESH,
        ).start()

    def drain(ref, sem):
        pltpu.make_async_copy(ref, ref, sem).wait()

    def send_group(src_of, dst, index):
        each_group(lambda t, xp, hp: start(
            src_of(t, xp, hp), dst.at[me], s_one.at[index], r_one.at[index], z * XN + xp, hp))
        pend.append(lambda: drain(dst.at[pl.ds(0, GN - 1)], s_one.at[index]))

    def recv_group(dst, index):
        drain(dst.at[pl.ds(0, GN - 1)], r_one.at[index])

    def send_x(src_of, dst, index):
        def step(i, carry):
            xp = (x + swing(i, XN)) % XN
            start(src_of(xp), dst.at[x], s_one.at[index], r_one.at[index], z * XN + xp, h)
            return carry
        lax.fori_loop(0, XN - 1, step, 0)
        pend.append(lambda: drain(dst.at[pl.ds(0, XN - 1)], s_one.at[index]))

    def recv_x(dst, index):
        drain(dst.at[pl.ds(0, XN - 1)], r_one.at[index])

    def send_z(src_of, dst, index, low, high):
        def act(zp):
            @pl.when((zp >= low) & (zp < high))
            def _():
                start(src_of(zp), dst.at[z], s_two.at[index, zp], r_two.at[index, z], zp * XN + x, h)
        each_z(act)
        pend.append(lambda: wait_z(dst, s_two, index, low, high))

    def wait_z(dst, sems, index, low, high):
        def step(zp, carry):
            @pl.when(zp != z)
            def _():
                drain(dst.at[zp], sems.at[index, zp])
            return carry
        lax.fori_loop(low, high, step, 0)

    loads[0].wait()
    loads[1].wait()
    upper, lower = features(k_ref[...], kw_ref[...])
    kf[:, :D] = upper
    kf[:, D:] = lower
    kh[...], kl[...] = split(kf[...])
    loads[2].wait()
    vh[:, :D], vl[:, :D] = split(v_ref[...])
    vh[:, D:] = jnp.ones((ROWS, D), BF16)
    vl[:, D:] = jnp.zeros((ROWS, D), BF16)
    tot = []
    for c in range(NC):
        r = pl.ds(c * CH, CH)
        st[c] = mm3((kh[r, :], kl[r, :]), (vh[r, :D], vl[r, :D]), TN)
        tot.append((jnp.sum(kf[r, :D], axis=0, keepdims=True), jnp.sum(kf[r, D:], axis=0, keepdims=True)))
    tot_all = jnp.concatenate([tot[0][0] + tot[1][0], tot[0][1] + tot[1][1]], axis=0)
    mine = st[0, pl.ds(h * (XN * TR), XN * TR), :] + st[1, pl.ds(h * (XN * TR), XN * TR), :]
    for i in range(XN):
        sa[i, :TR] = mine[TR * i:TR * i + TR]
        sa[i, TR:TM] = tot_all
    @pl.when(core == 0)
    def _():
        pl.semaphore_wait(barrier, 2 * (XN - 1) + 1)
        pl.semaphore_signal(ready.at[0], inc=1, device_id=(pos, first + 1), device_id_type=MESH)

    @pl.when(core == 1)
    def _():
        pl.semaphore_wait(ready.at[0], 1)
    send_x(lambda xp: sa.at[xp, pl.ds(0, TM)], ra.at[:, pl.ds(0, TM)], 0)
    ra[x] = sa[x]

    for load in loads[3:]:
        load.wait()
    kth[...], ktl[...] = split(jnp.transpose(k_ref[...]))

    ids = ids_ref[...]
    onehot = (lax.broadcasted_iota(jnp.int32, (64, ROWS), 0) == ids).astype(F32).astype(BF16)
    diag = lax.broadcasted_iota(jnp.int32, (64, 64), 0) == lax.broadcasted_iota(jnp.int32, (64, 64), 1)
    wcol = jnp.sum(jnp.where(diag, sw_ref[...], 0.0), axis=1, keepdims=True)
    wtab = jnp.broadcast_to(wcol, (64, D))
    w1, rest = wtab.astype(BF16), wtab - wtab.astype(BF16).astype(F32)
    w2, w3 = split(rest)
    weight = dot(onehot, w1, TN) + dot(onehot, w2, TN) + dot(onehot, w3, TN)
    mask = lax.broadcasted_iota(jnp.int32, (CH, CH), 0) >= lax.broadcasted_iota(jnp.int32, (CH, CH), 1)

    def before(n):
        lanes = pl.ds(n * D, D)
        scaled[n] = c_ref[:, lanes] * weight
        upper, lower = features(q_ref[:, lanes], qw_ref[n])
        qf[n, :, :D] = upper
        qf[n, :, D:] = lower
        qh[n], ql[n] = split(qf[n])
        qth[n], qtl[n] = split(jnp.transpose(qf[n]))
        for c in range(NC):
            r = pl.ds(c * CH, CH)
            s = mm3((qh[n, r, :], ql[n, r, :]), (kh[r, :], kl[r, :]), NT)
            sh[n, r, :], sl[n, r, :] = split(jnp.where(mask, s, 0.0))
            intra[n, r, :] = mm3((sh[n, r, :], sl[n, r, :]), (vh[r, :], vl[r, :]), NN)

    @pl.when(core == 1)
    def _():
        pl.semaphore_wait(barrier, 2 * (ZN - 1) + GN - 1)
        pl.semaphore_signal(ready.at[1], inc=1, device_id=(pos, first), device_id_type=MESH)

    @pl.when(core == 0)
    def _():
        pl.semaphore_wait(ready.at[1], 1)
    recv_x(ra.at[:, pl.ds(0, TM)], 0)
    ta[...] = total(ra)
    send_z(lambda zp: ta.at[pl.ds(0, TM)], za.at[:, pl.ds(0, TM)], 0, z + 1, ZN)
    before(0)
    before(1)
    wait_z(za.at[:, pl.ds(0, TM)], r_two, 0, 0, z)
    pre = jnp.sum(za[...], axis=0)
    pre_tot = pre[TR:TM]
    for i in range(XN):
        gas[i] = pre[:TR]
        if i < XN - 1:
            pre = pre + ra[i]
            pre_tot = pre_tot + jnp.where(i < x, ra[i, TR:TM], 0.0)
    send_group(lambda t, xp, hp: gas.at[xp], ga, 1)
    ga[me] = gas[x]

    totals = [(pre_tot[0:1], pre_tot[1:2])]
    for c in range(1, NC):
        totals.append((totals[c - 1][0] + tot[c - 1][0], totals[c - 1][1] + tot[c - 1][1]))
    carried = []
    for c in range(NC):
        r = pl.ds(c * CH, CH)
        col = split(jnp.concatenate([column(totals[c][0]), column(totals[c][1])], axis=0))
        acc = None
        for n in range(2):
            inv = 1.0 / (intra[n, r, D:] + mm3((qh[n, r, :], ql[n, r, :]), col, NN))
            invs[n, r, :] = inv
            g = split(scaled[n, r, :] * inv)
            gnh[n, r, :], gnl[n, r, :] = g
            term = mm3((qth[n, :, r], qtl[n, :, r]), g, NN)
            acc = term if acc is None else acc + term
        carried.append(acc)
    c1[...] = carried[1]
    whole = carried[0] + carried[1]
    for t in range(GN):
        cb[t] = whole[TR * t:TR * t + TR]
    send_group(lambda t, xp, hp: cb.at[t], rb, 2)
    rb[me] = cb[me]

    recv_group(ga, 1)
    p_now = ga[...].reshape(2 * D, D)
    states = []
    for c in range(NC):
        states.append(split(p_now))
        if c < NC - 1:
            p_now = p_now + st[c]
    ct = [[0.0, 0.0] for _ in range(NC)]
    for c in range(NC):
        r = pl.ds(c * CH, CH)
        for n in range(2):
            num = intra[n, r, :D] + mm3((qh[n, r, :], ql[n, r, :]), states[c], NN)
            inv = invs[n, r, :]
            gno = -jnp.sum(scaled[n, r, :] * (num * inv), axis=1, keepdims=True) * inv
            gnorm[n, r, :] = gno
            ct[c][0] = ct[c][0] + jnp.sum(gno * qf[n, r, :D], axis=0, keepdims=True)
            ct[c][1] = ct[c][1] + jnp.sum(gno * qf[n, r, D:], axis=0, keepdims=True)
    ctb[...] = jnp.concatenate([ct[0][0] + ct[1][0], ct[0][1] + ct[1][1]], axis=0)
    send_group(lambda t, xp, hp: ctb, ctr, 10)
    ctr[me] = ctb[...]

    grads = [[], []]

    def after(n, parts):
        lanes = pl.ds(n * D, D)
        wpair = split(qw_ref[n])
        for c in parts:
            r = pl.ds(c * CH, CH)
            g = (gnh[n, r, :], gnl[n, r, :])
            gno = gnorm[n, r, :]
            gs = mm3(g, (vh[r, :D], vl[r, :D]), NT) + jnp.concatenate([gno, gno], axis=1)
            gs = split(jnp.where(mask, gs, 0.0))
            gfeat = mm3(gs, (kh[r, :], kl[r, :]), NN) + mm3(g, states[c], NT)
            a = gfeat[:, :D] + gno * totals[c][0]
            b = gfeat[:, D:] + gno * totals[c][1]
            gl = split(back(qf[n, r, :D], qf[n, r, D:], a, b))
            grads[n].append(gl)
            gq_ref[r, lanes] = mm3(gl, wpair, NT)
            gk = mm3(gs, (qh[n, r, :], ql[n, r, :]), TN)
            gv = mm3((sh[n, r, :], sl[n, r, :]), g, TN)
            if n == 0:
                gkf[r, :] = gk
                gval[r, :] = gv
            else:
                gkf[r, :] += gk
                gval[r, :] += gv

    def weight_grad(n):
        gl = tuple(jnp.concatenate([g[i] for g in grads[n]], axis=0) for i in range(2))
        gw = mm3(split(q_ref[:, n * D:n * D + D]), gl, TN)
        parts = XN // 2
        for i in range(parts):
            qs[parts * n + i] = gw[QX * i:QX * i + QX]

    def over_heads(ref):
        sums = []
        for i in range(XN):
            acc = ref[i]
            for hp in range(1, HN):
                acc = acc + ref[hp * XN + i]
            sums.append(acc)
        return sums

    recv_group(rb, 2)
    by_x = over_heads(rb)
    tb[...] = total(by_x)
    send_z(lambda zp: tb, zb, 1, 0, z)
    after(0, (0, 1))
    after(1, (0,))
    recv_group(ctr, 10)
    ct_x = over_heads(ctr)
    ctt[...] = total(ct_x)
    send_z(lambda zp: ctt, zct, 5, 0, z)
    after(1, (1,))
    stores[0].start()

    wait_z(zb, r_two, 1, z + 1, ZN)
    suf = jnp.sum(zb[...], axis=0)
    for i in reversed(range(XN)):
        gbs[i] = suf
        if i > 0:
            suf = suf + by_x[i]
    send_group(lambda t, xp, hp: gbs.at[xp], gb, 4)
    gb[me] = gbs[x]
    weight_grad(0)
    weight_grad(1)
    send_x(lambda xp: qs.at[xp], rq, 3)
    rq[x] = qs[x]

    r = pl.ds(0, CH)
    cpair = split(c1[...])
    gkf[r, :] += mm3((vh[r, :D], vl[r, :D]), cpair, NT) + jnp.concatenate([ct[1][0], ct[1][1]], axis=1)
    gval[r, :] += mm3((kh[r, :], kl[r, :]), cpair, NN)
    gl = back(kf[:, :D], kf[:, D:], gkf[:, :D], gkf[:, D:])
    for i in range(HN):
        ks[i, :, :D] = gl[OWN * i:OWN * i + OWN]
        ks[i, :, D:] = gval[OWN * i:OWN * i + OWN, :]

    kpair = (kth[...], ktl[...])
    gkw = mm3(kpair, split(gl), NN)
    for i in range(GN):
        iks[i] = gkw[KW * i:KW * i + KW]
    send_group(lambda t, xp, hp: iks.at[t], ikr, 9)
    ikr[me] = iks[me]

    recv_x(rq, 3)
    tsum = total(rq)
    for i in range(ZN):
        tq[i] = tsum[QZ * i:QZ * i + QZ]
    send_z(lambda zp: tq.at[zp], zq, 2, 0, ZN)
    zq[z] = tq[z]
    recv_group(ikr, 9)
    early = jnp.sum(ikr[...], axis=0)

    recv_group(gb, 4)
    wait_z(zct, r_two, 5, z + 1, ZN)
    suf_tot = jnp.sum(zct[...], axis=0)
    for i in range(1, XN):
        suf_tot = suf_tot + jnp.where(i > x, ct_x[i], 0.0)
    later = split(gb[...].reshape(2 * D, D))
    gfeat = mm3((vh[:, :D], vl[:, :D]), later, NT)
    gl = back(kf[:, :D], kf[:, D:], gfeat[:, :D] + suf_tot[0:1], gfeat[:, D:] + suf_tot[1:2])
    gkw = mm3(kpair, split(gl), NN)
    for i in range(GN):
        ck[i] = gkw[KW * i:KW * i + KW]
    send_x(lambda xp: ck.at[h * XN + xp], rc, 6)
    rc[x] = ck[me]
    gint[...] = gl

    def send_key(i, carry):
        hp = (h + i) % HN
        start(ks.at[hp], kr.at[h], s_one.at[5], r_one.at[5], pos, hp)
        return carry
    lax.fori_loop(1, HN, send_key, 0)
    pend.append(lambda: drain(kr.at[pl.ds(0, HN - 1)], s_one.at[5]))
    kr[h] = ks[h]

    wait_z(zq, r_two, 2, 0, ZN)
    gzs[...] = jnp.sum(zq[...], axis=0)
    send_z(lambda zp: gzs, gz, 3, 0, ZN)
    gz[z] = gzs[...]

    recv_x(rc, 6)
    tc[...] = total(rc) + early
    send_z(lambda zp: tc, zc, 4, 0, ZN)
    zc[z] = tc[...]

    wait_z(gz, r_two, 3, 0, ZN)
    send_x(lambda xp: gz, gx, 7)
    gx[x] = gz[...]

    wait_z(zc, r_two, 4, 0, ZN)
    gcs[...] = jnp.sum(zc[...], axis=0)
    send_group(lambda t, xp, hp: gcs, gc, 8)
    gc[me] = gcs[...]
    last = pend.pop()

    recv_x(gx, 7)
    for i in range(XN):
        for j in range(ZN):
            row = QX * i + QZ * j
            gqw_ref[row // D, row % D:row % D + QZ, :] = gx[i, j]
    stores[3].start()
    own = pl.ds(h * OWN, OWN)
    drain(kr.at[pl.ds(0, HN - 1)], r_one.at[5])
    got = kr[0]
    for i in range(1, HN):
        got = got + kr[i]
    gk_ref[...] = mm3(split(gint[own, :] + got[:, :D]), split(kw_ref[...]), NT)
    gv_ref[...] = mm3((kh[own, :], kl[own, :]), later, NN) + got[:, D:]
    stores[1].start()
    stores[2].start()
    finish()
    recv_group(gc, 8)
    for i in range(GN):
        gkw_ref[KW * i:KW * i + KW, :] = gc[i]
    stores[4].start()
    last()
    for copy in stores:
        copy.wait()


def store(*refs):
    sources, targets, held, sems = refs[:5], refs[5:10], refs[10:15], refs[15]
    reads = [pltpu.make_async_copy(sources[i], held[i], sems.at[0, i]) for i in range(5)]
    writes = [pltpu.make_async_copy(held[i], targets[i], sems.at[1, i]) for i in range(5)]
    for read in reads:
        read.start()
    for read, write in zip(reads, writes):
        read.wait()
        write.start()
    for write in writes:
        write.wait()


def on_device(queries, keys, values, cotangent, source_ids, source_weights, q_feature, k_feature):
    def vm(*shape, dtype=F32):
        return pltpu.VMEM(shape, dtype)

    b = dict(dtype=BF16)
    results = pl.pallas_call(
        kernel,
        out_shape=(
            jax.ShapeDtypeStruct((ROWS, 2 * D), F32),
            jax.ShapeDtypeStruct((OWN, D), F32),
            jax.ShapeDtypeStruct((OWN, D), F32),
            jax.ShapeDtypeStruct((2, D, D), F32),
            jax.ShapeDtypeStruct((D, D), F32),
        ),
        in_specs=[pl.BlockSpec(memory_space=pl.ANY)] * 8,
        out_specs=[pl.BlockSpec(memory_space=pl.ANY)] * 5,
        scratch_shapes=[
            vm(ROWS, 2 * D), vm(OWN, D), vm(OWN, D), vm(2, D, D), vm(D, D), pltpu.SemaphoreType.DMA((5,)),
            vm(ROWS, 2 * D), vm(ROWS, D), vm(ROWS, D), vm(ROWS, 2 * D), vm(1, ROWS, dtype=jnp.int32), vm(1, 64),
            vm(2, D, D), vm(D, D), pltpu.SemaphoreType.DMA((8,)),
            vm(ROWS, 2 * D), vm(ROWS, 2 * D, **b), vm(ROWS, 2 * D, **b),
            vm(ROWS, 2 * D, **b), vm(ROWS, 2 * D, **b),
            vm(2, ROWS, 2 * D), vm(2, ROWS, 2 * D, **b), vm(2, ROWS, 2 * D, **b),
            vm(2, ROWS, CH, **b), vm(2, ROWS, CH, **b),
            vm(2, ROWS, 2 * D), vm(2, ROWS, D), vm(NC, 2 * D, D),
            vm(2, ROWS, D, **b), vm(2, ROWS, D, **b), vm(2, ROWS, D),
            vm(2 * D, D), vm(ROWS, 2 * D), vm(ROWS, D),
            vm(XN, TP, D), vm(XN, TP, D), vm(TP, D), vm(ZN, TP, D), vm(XN, TR, D), vm(GN, TR, D),
            vm(GN, TR, D), vm(GN, TR, D), vm(TR, D), vm(ZN, TR, D), vm(XN, TR, D), vm(GN, TR, D),
            vm(HN, OWN, 2 * D), vm(HN, OWN, 2 * D),
            vm(XN, QX, D), vm(XN, QX, D), vm(ZN, QZ, D), vm(ZN, QZ, D),
            vm(QZ, D), vm(ZN, QZ, D), vm(XN, ZN, QZ, D),
            vm(GN, KW, D), vm(XN, KW, D), vm(KW, D), vm(ZN, KW, D), vm(KW, D), vm(GN, KW, D),
            vm(2, 2 * D, ROWS, **b), vm(2, 2 * D, ROWS, **b), vm(D, ROWS, **b), vm(D, ROWS, **b),
            vm(GN, KW, D), vm(GN, KW, D), vm(ROWS, D),
            vm(2, ROWS, D), vm(2, D), vm(GN, 2, D), vm(2, D), vm(ZN, 2, D),
            pltpu.SemaphoreType.DMA((11,)),
            pltpu.SemaphoreType.DMA((6, ZN)),
            pltpu.SemaphoreType.DMA((11,)),
            pltpu.SemaphoreType.DMA((6, ZN)),
            pltpu.SemaphoreType.REGULAR((2,)),
        ],
        compiler_params=pltpu.CompilerParams(
            collective_id=0, has_side_effects=True, vmem_limit_bytes=60 * 1024 * 1024
        ),
        cost_estimate=pl.CostEstimate(flops=3_000_000_000, bytes_accessed=2_500_000, transcendentals=400_000),
    )(queries, keys, values, cotangent, source_ids.reshape(1, ROWS), source_weights.reshape(1, -1), q_feature, k_feature)
    return pl.pallas_call(
        store,
        out_shape=[jax.ShapeDtypeStruct(a.shape, a.dtype) for a in results],
        in_specs=[pl.BlockSpec(memory_space=pl.ANY)] * 5,
        out_specs=[pl.BlockSpec(memory_space=pl.ANY)] * 5,
        scratch_shapes=[pltpu.VMEM(a.shape, a.dtype) for a in results] + [pltpu.SemaphoreType.DMA((2, 5))],
        compiler_params=pltpu.CompilerParams(vmem_limit_bytes=60 * 1024 * 1024),
    )(*results)


def solution(mesh):
    placed = (
        P("ctx", "head"),
        P("ctx", None),
        P("ctx", None),
        P("ctx", "head"),
        P("ctx"),
        P(),
        P("head", None, None),
        P(),
    )
    return jax.shard_map(
        on_device,
        mesh=mesh,
        in_specs=placed,
        out_specs=(
            P("ctx", "head"),
            P(("ctx", "head"), None),
            P(("ctx", "head"), None),
            P("head", None, None),
            P(),
        ),
        check_vma=False,
    )
```
